128 devices in a mesh: seq: 16 (over z_hi, x, core), head: 8 (over z_lo, y).
Axes of the slice: x: 4, y: 4, z: 4 (z_hi: 2, z_lo: 2; z = z_hi * 2 + z_lo), core: 2. Of those that a mesh axis runs over, the one named last changes fastest.
Arguments:
- queries: bfloat16 [65536, 512], P('seq'), may hold values from -250 to 250
- memory: bfloat16 [2048, 1024], replicated, may hold values from -6 to 6
- w_query: bfloat16 [512, 512], P(None, 'head'), may hold values from -0.25 to 0.25
- w_key: bfloat16 [1024, 512], P(None, 'head'), may hold values from -0.1875 to 0.1875
- w_value: bfloat16 [1024, 512], P(None, 'head'), may hold values from -0.1875 to 0.1875
- w_out: bfloat16 [512, 512], P('head'), may hold values from -0.25 to 0.25
- grad_out: bfloat16 [65536, 512], P('seq'), may hold values from -384 to 384
- masked: int32 [65536], P('seq'), may hold values from 0 to 1, as said below
Outputs:
- grad_wq: float32 [512, 512], P('seq', 'head')
- grad_wk: float32 [1024, 512], P('seq', 'head')
- grad_wv: float32 [1024, 512], P('seq', 'head')
- grad_wo: float32 [512, 512], P('head', 'seq')
- grad_memory: float32 [2048, 1024], P('seq', 'head')
The draws below stay inside these ranges and needn't reach their ends.
Inputs may be any that keep to these rules, and one draw needn't show every extreme that they name: The first position of every block of 4096 bytes is masked.
All inputs are finite; a program needn't handle non-finite values.
Results may differ from the reference program's by a relative error of at most 0.033.
Values sent between devices are 32-bit elements; how exact they have to be, the bound alone decides.
No kernel may reach another device: no remote copies, remote signals or barrier semaphores. Data moves between devices by JAX's collectives and lax.ppermute only.
A program may use at most 64 MiB of HBM per device.

```python
import jax
import jax.numpy as jnp
from jax import lax

E = 512
C = 1024
L = 2048
H = 8
DH = 64
QDEV = 4096
TOKENS = 65536


def draw_queries(key, part):
    key = jax.random.fold_in(key, 11)
    base = jax.random.normal(key, (TOKENS, E), jnp.float32)
    return jnp.clip(base, -250.0, 250.0).astype(jnp.bfloat16)


def draw_masked(key, part):
    key = jax.random.fold_in(key, 23)
    ticket = jax.random.randint(key, (TOKENS,), 0, 1000)
    position = jnp.arange(TOKENS)
    limit = 100 + 200 * position // TOKENS
    chosen = (ticket < limit) | (position % QDEV == 0)
    return chosen.astype(jnp.int32)


def shard_levels(own_key, dims, cuts, smallest, high):
    factor_of, own = 1.0, jax.random.fold_in(own_key, 6)
    for dim, blocks in cuts:
        heights = jnp.exp(jax.random.uniform(jax.random.fold_in(own, dim), (blocks,), jnp.float32, smallest / len(cuts), high / len(cuts)))
        factor_of = factor_of * jnp.repeat(heights, dims[dim] // blocks).reshape([-1 if axis == dim else 1 for axis in range(len(dims))])
    return factor_of


def normal_values(own_key, shape, spread, bound, shards=(), dtype=jnp.bfloat16):
    loudness = shard_levels(own_key, shape, shards, -0.22, 0.18) if shards else 1.0
    drawn = jax.random.normal(own_key, shape, jnp.float32) * spread * loudness
    return jnp.minimum(jnp.maximum(drawn, -bound), bound).astype(dtype)


def setup_inputs(seed: int = 0) -> dict:
    streams_of = jax.random.split(jax.random.key(seed), 9)
    return {
        "queries": draw_queries(jax.random.fold_in(streams_of[8], 71), 0),
        "memory": normal_values(streams_of[1], (L, C), 1.0, 6.0),
        "w_query": normal_values(streams_of[2], (E, H * DH), E ** -0.5, 0.25, ((1, 8),)),
        "w_key": normal_values(streams_of[3], (C, H * DH), C ** -0.5, 0.1875, ((1, 8),)),
        "w_value": normal_values(streams_of[4], (C, H * DH), C ** -0.5, 0.1875, ((1, 8),)),
        "w_out": normal_values(streams_of[5], (H * DH, E), (H * DH) ** -0.5, 0.25, ((0, 8),)),
        "grad_out": normal_values(streams_of[6], (TOKENS, E), 64.0, 384.0, ((0, 16),)),
        "masked": draw_masked(jax.random.fold_in(streams_of[8], 71), 0),
    }


def reference(queries, memory, w_query, w_key, w_value, w_out, grad_out, masked):
    f32 = jnp.float32
    bf16 = jnp.bfloat16
    mask_total = jnp.sum(masked).astype(f32)
    weighted = grad_out * masked[:, None].astype(bf16)
    key_proj = jnp.dot(memory, w_key, preferred_element_type=f32).astype(bf16).reshape(L, H, DH)
    value_proj = jnp.dot(memory, w_value, preferred_element_type=f32).astype(bf16).reshape(L, H, DH)
    block_rows = 1024 if TOKENS % 1024 == 0 else TOKENS
    block_count = TOKENS // block_rows
    key_f = key_proj.astype(f32)
    value_f = value_proj.astype(f32)

    def fold_block(carried, inputs_pair):
        acc_key, acc_value, acc_query, acc_out = carried
        tokens, grads = inputs_pair
        query_proj = jnp.dot(tokens, w_query, preferred_element_type=f32).astype(bf16)
        query_three = query_proj.reshape(block_rows, H, DH).astype(f32)
        score_block = jnp.einsum('qhd,khd->hqk', query_three, key_f) * 0.125
        top_score = jnp.max(score_block, axis=-1, keepdims=True)
        expo_block = jnp.exp(score_block - top_score)
        prob_block = expo_block / jnp.sum(expo_block, axis=-1, keepdims=True)
        prob_b = prob_block.astype(bf16).astype(f32)
        attended = jnp.einsum('hqk,khd->qhd', prob_b, value_f).astype(bf16)
        flat_att = attended.reshape(block_rows, H * DH)
        d_attended = jnp.dot(grads, w_out.T, preferred_element_type=f32).astype(bf16)
        acc_out = acc_out + jnp.dot(flat_att.T, grads, preferred_element_type=f32)
        d_three = d_attended.reshape(block_rows, H, DH).astype(f32)
        d_prob = jnp.einsum('qhd,khd->hqk', d_three, value_f)
        row_delta = jnp.einsum('qhd,qhd->hq', d_three, attended.astype(f32))
        d_score = (prob_block * (d_prob - row_delta[:, :, None]) * 0.125).astype(bf16).astype(f32)
        d_query = jnp.einsum('hqk,khd->qhd', d_score, key_f).astype(bf16).reshape(block_rows, H * DH)
        acc_query = acc_query + jnp.dot(tokens.T, d_query, preferred_element_type=f32)
        acc_key = acc_key + jnp.einsum('hqk,qhd->khd', d_score, query_three)
        acc_value = acc_value + jnp.einsum('hqk,qhd->khd', prob_b, d_three)
        return (acc_key, acc_value, acc_query, acc_out), None

    start = (jnp.zeros((L, H, DH), f32), jnp.zeros((L, H, DH), f32),
             jnp.zeros((E, H * DH), f32), jnp.zeros((H * DH, E), f32))
    pairs = (queries.reshape(block_count, block_rows, E), weighted.reshape(block_count, block_rows, E))
    (acc_key, acc_value, acc_query, acc_out), _ = lax.scan(fold_block, start, pairs)
    grad_wq = acc_query / mask_total
    grad_wo = acc_out / mask_total
    d_key = (acc_key / mask_total).astype(bf16).reshape(L, H * DH)
    d_value = (acc_value / mask_total).astype(bf16).reshape(L, H * DH)
    grad_wk = jnp.dot(memory.T, d_key, preferred_element_type=f32)
    grad_wv = jnp.dot(memory.T, d_value, preferred_element_type=f32)
    grad_memory = jnp.dot(d_key, w_key.T, preferred_element_type=f32) + jnp.dot(d_value, w_value.T, preferred_element_type=f32)
    return (grad_wq, grad_wk, grad_wv, grad_wo, grad_memory)
```

```python
import functools

import jax
import jax.numpy as jnp
from jax import lax
from jax.experimental import pallas as pl
from jax.experimental.pallas import tpu as pltpu
from jax.sharding import PartitionSpec as P

DH = 64
ROWS = 4096
LAT = 2048
E = 512
C = 1024
PACK = 256
SMALL = 128
LARGE = 272
TB = 256
MEM_PARTS = 4
ROW_PARTS = 4
f32 = jnp.float32
bf16 = jnp.bfloat16


def _dot(a, b, dims):
    return lax.dot_general(a, b, (dims, ((), ())), preferred_element_type=f32)


NN = ((1,), (0,))
NT = ((1,), (1,))


def main_kernel(
    sidx, masked, q_hbm, g_hbm, mem_hbm, wq_hbm, wk_hbm, wv_hbm, wo_hbm,
    keep_a, send_a, keep_b, send_b,
    q_in, g_in, mem, wq, wk, wv, wo, qc, gc, kv, wkv, wq2, wo2, pos, off_v, off_s,
    dkv, wqo, wkv_out, wqo_out,
    mem_sem, row_sem, w_sem, off_sem,
):
    me = sidx[0]
    w_copies = [
        pltpu.make_async_copy(src, dst, w_sem.at[i])
        for i, (src, dst) in enumerate(((wk_hbm, wk), (wv_hbm, wv), (wq_hbm, wq), (wo_hbm, wo)))
    ]
    mrows = LAT // MEM_PARTS
    mem_copies = [
        pltpu.make_async_copy(
            mem_hbm.at[pl.ds(i * mrows, mrows)], mem.at[pl.ds(i * mrows, mrows)], mem_sem.at[i]
        )
        for i in range(MEM_PARTS)
    ]
    rrows = ROWS // ROW_PARTS
    row_copies = [
        [
            pltpu.make_async_copy(
                src.at[pl.ds(i * rrows, rrows)], dst.at[pl.ds(i * rrows, rrows)], row_sem.at[2 * i + j]
            )
            for j, (src, dst) in enumerate(((q_hbm, q_in), (g_hbm, g_in)))
        ]
        for i in range(ROW_PARTS)
    ]
    for c in w_copies + mem_copies:
        c.start()
    for pair in row_copies:
        for c in pair:
            c.start()

    ones = masked[...].astype(f32)
    mb = ones.astype(bf16)
    r128 = lax.broadcasted_iota(jnp.int32, (128, 128), 0)
    c128 = lax.broadcasted_iota(jnp.int32, (128, 128), 1)
    before = (r128 < c128).astype(f32).astype(bf16)
    rank = _dot(mb, before, NN)
    counts = _dot(mb, jnp.ones((128, 128), bf16), NN)
    r40 = lax.broadcasted_iota(jnp.int32, (40, 32), 0)
    c40 = lax.broadcasted_iota(jnp.int32, (40, 32), 1)
    earlier = (c40 < r40).astype(f32).astype(bf16)
    offs = _dot(earlier, counts.astype(bf16), NN)
    off_v[...] = offs.astype(jnp.int32)
    off_copy = pltpu.make_async_copy(off_v, off_s, off_sem)
    off_copy.start()
    pos[...] = jnp.where(ones > 0.5, offs[:32] + rank, -1.0).astype(jnp.int32)

    dkv[...] = jnp.zeros_like(dkv)
    wqo[...] = jnp.zeros_like(wqo)
    qc[pl.ds(0, 16), :] = jnp.zeros((16, E), bf16)
    gc[pl.ds(0, 16), :] = jnp.zeros((16, E), bf16)

    for c in w_copies:
        c.wait()
    wkv[:, :DH] = wk[...]
    wkv[:, DH:] = wv[...]
    wq2[:, :DH] = wq[...]
    wq2[:, DH:] = jnp.zeros((E, DH), bf16)
    wo2[:DH, :] = jnp.zeros((DH, E), bf16)
    wo2[DH:, :] = wo[...]
    for i, c in enumerate(mem_copies):
        c.wait()
        part = pl.ds(i * mrows, mrows)
        kv[part, :] = _dot(mem[part, :], wkv[...], NN).astype(bf16)

    off_copy.wait()
    total = off_s[32, 0]

    def put(b, start, size):
        row = lax.broadcasted_iota(jnp.int32, (size, 128), 0) + start
        picks = [
            (row == pos[pl.ds(2 * b + half, 1), :]).astype(f32).astype(bf16) for half in range(2)
        ]
        pick = jnp.concatenate(picks, axis=1)
        src = pl.ds(b * PACK, PACK)
        first = pl.ds(start, 16)
        rest = pl.ds(pl.multiple_of(start + 16, 16), size - 16)
        for s_ref, d_ref in ((q_in, qc), (g_in, gc)):
            rows = _dot(pick, s_ref[src, :], NN)
            d_ref[first, :] = (rows[:16] + d_ref[first, :].astype(f32)).astype(bf16)
            d_ref[rest, :] = rows[16:].astype(bf16)

    per = rrows // PACK
    for b in range(ROWS // PACK):
        if b % per == 0:
            for c in row_copies[b // per]:
                c.wait()
        base = off_s[2 * b, 0]
        nxt = off_s[2 * b + 2, 0]
        start = pl.multiple_of((base // 16) * 16, 16)
        few = nxt - start < SMALL
        pl.when(few)(functools.partial(put, b, start, SMALL))
        pl.when(jnp.logical_not(few))(functools.partial(put, b, start, LARGE))

    tail = pl.ds(pl.multiple_of(((total + 15) // 16) * 16, 16), TB)
    qc[tail, :] = jnp.zeros((TB, E), bf16)
    gc[tail, :] = jnp.zeros((TB, E), bf16)

    def block(i, _):
        rows = pl.ds(pl.multiple_of(i * TB, TB), TB)
        q = qc[rows, :]
        g = gc[rows, :]
        qp = _dot(q, wq2[...], NN).astype(bf16).astype(f32) * 0.125
        da = _dot(g, wo2[...], NT).astype(bf16)
        score = _dot(qp.astype(bf16), kv[...], NT)
        dprob = _dot(da, kv[...], NT)
        top = jnp.max(score, axis=1, keepdims=True)
        e = jnp.exp(score - top)
        inv = 1.0 / jnp.sum(e, axis=1, keepdims=True)
        eb = e.astype(bf16)
        att = (_dot(eb, kv[...], NN) * inv).astype(bf16)
        daf = da.astype(f32)
        delta = jnp.sum(daf * att.astype(f32), axis=1, keepdims=True)
        ds = (e * (dprob - delta)).astype(bf16)
        dq = _dot(ds, kv[...], NN) * (inv * 0.125)
        lane = lax.broadcasted_iota(jnp.int32, (TB, 128), 1)
        x = jnp.where(lane < DH, dq, att.astype(f32))
        y = (qp + daf) * inv
        xt = x.T.astype(bf16)
        yt = y.T.astype(bf16)
        wqo[:DH, :] += _dot(xt[:DH], q, NN)
        wqo[DH:, :] += _dot(xt[DH:], g, NN)
        dkv[:DH, :] += _dot(yt[:DH], ds, NN)
        dkv[DH:, :] += _dot(yt[DH:], eb, NN)
        return 0

    lax.fori_loop(0, (total + TB - 1) // TB, block, 0)

    wkvt = _dot(dkv[...].astype(bf16), mem[...], NN)
    lane64 = lax.broadcasted_iota(jnp.int32, (64, 128), 1)
    for t in range(8):
        tk = wkvt[:DH, 128 * t : 128 * (t + 1)]
        tv = wkvt[DH:, 128 * t : 128 * (t + 1)]
        wkv_out[2 * t] = jnp.where(lane64 < DH, tk, pltpu.roll(tv, 64, 1))
        wkv_out[2 * t + 1] = jnp.where(lane64 < DH, pltpu.roll(tk, 64, 1), tv)
    lane32 = lax.broadcasted_iota(jnp.int32, (32, 128), 1)
    for t in range(4):
        cols = slice(128 * t, 128 * (t + 1))
        for u in range(4):
            chunk = None
            for k, lo in ((0, 0), (1, 64), (2, 32), (3, 96)):
                piece = wqo[lo : lo + 32, cols]
                shift = (32 * (k - u)) % 128
                piece = pltpu.roll(piece, shift, 1) if shift else piece
                chunk = piece if chunk is None else jnp.where(lane32 >= 32 * k, piece, chunk)
            wqo_out[4 * t + u] = chunk
    count = jnp.zeros((8, 128), f32) + total.astype(f32)
    for p in range(16):
        rc, rx, rz = p // 8, (p // 2) % 4, p % 2
        s = me ^ (rz * 8 + rx * 2 + rc)
        a = (keep_a, send_a)[rc]
        b = (keep_b, send_b)[rc]
        i = p % 8
        a[i] = dkv[:, pl.ds(pl.multiple_of(s * 128, 128), 128)]
        b[i, 0:64] = wkv_out[s]
        b[i, 64:96] = wqo_out[s]
        b[i, 96:104] = count


def run_main(sidx, masked, queries, grads, memory, w_query, w_key, w_value, w_out):
    any_ = pl.BlockSpec(memory_space=pl.ANY)
    vm = pl.BlockSpec(memory_space=pltpu.VMEM)
    a = jax.ShapeDtypeStruct((8, 128, 128), f32)
    b = jax.ShapeDtypeStruct((8, 104, 128), f32)
    pad = ROWS + LARGE + TB
    return pl.pallas_call(
        main_kernel,
        out_shape=(a, a, b, b),
        in_specs=[pl.BlockSpec(memory_space=pltpu.SMEM), vm] + [any_] * 7,
        out_specs=(vm,) * 4,
        scratch_shapes=[
            pltpu.VMEM((ROWS, E), bf16),
            pltpu.VMEM((ROWS, E), bf16),
            pltpu.VMEM((LAT, C), bf16),
            pltpu.VMEM((E, DH), bf16),
            pltpu.VMEM((C, DH), bf16),
            pltpu.VMEM((C, DH), bf16),
            pltpu.VMEM((DH, E), bf16),
            pltpu.VMEM((pad, E), bf16),
            pltpu.VMEM((pad, E), bf16),
            pltpu.VMEM((LAT, 128), bf16),
            pltpu.VMEM((C, 128), bf16),
            pltpu.VMEM((E, 128), bf16),
            pltpu.VMEM((128, E), bf16),
            pltpu.VMEM((32, 128), jnp.int32),
            pltpu.VMEM((40, 128), jnp.int32),
            pltpu.SMEM((40, 128), jnp.int32),
            pltpu.VMEM((128, LAT), f32),
            pltpu.VMEM((128, E), f32),
            pltpu.VMEM((16, 64, 128), f32),
            pltpu.VMEM((16, 32, 128), f32),
            pltpu.SemaphoreType.DMA((MEM_PARTS,)),
            pltpu.SemaphoreType.DMA((2 * ROW_PARTS,)),
            pltpu.SemaphoreType.DMA((4,)),
            pltpu.SemaphoreType.DMA(()),
        ],
        compiler_params=pltpu.CompilerParams(vmem_limit_bytes=60 * 1024 * 1024),
        cost_estimate=pl.CostEstimate(flops=10**10, bytes_accessed=14 * 2**20, transcendentals=10**7),
        name="masked_rows",
    )(sidx, masked, queries, grads, memory, w_query, w_key, w_value, w_out)


def head_kernel(hidx, part0, part1, wk, wv, keep_al, send_al, keep_be, send_be):
    me = hidx[0]
    d = (part0[...] + part1[...]).astype(bf16)
    dt = d.T
    for ry in range(4):
        for rz in range(2):
            c = me ^ (rz * 4 + ry)
            rows = pl.ds(pl.multiple_of(c * 128, 128), 128)
            w = jnp.concatenate([wk[rows, :], wv[rows, :]], axis=1)
            out = _dot(dt, w, NT)
            al = (keep_al, 0) if ry == 0 else (keep_al, 1) if ry == 3 else (send_al, ry - 1)
            be = (keep_be, ry) if ry < 2 else (send_be, 3 - ry)
            al[0][al[1], rz] = out[:64]
            be[0][be[1], rz] = out[64:]


def run_head(hidx, part0, part1, w_key, w_value):
    vm = pl.BlockSpec(memory_space=pltpu.VMEM)
    o = jax.ShapeDtypeStruct((2, 2, 64, 128), f32)
    return pl.pallas_call(
        head_kernel,
        out_shape=(o,) * 4,
        in_specs=[pl.BlockSpec(memory_space=pltpu.SMEM)] + [vm] * 4,
        out_specs=(vm,) * 4,
        name="memory_part",
    )(hidx, part0, part1, w_key, w_value)


def swap(x, axis, bits):
    n = lax.axis_size(axis)
    return lax.ppermute(x, axis, [(i, i ^ bits) for i in range(n)])


def ring_reduce(al_keep, al_send, be_keep, be_send, axis, near, far):
    al_in = swap(al_send, axis, near)
    be_in = swap(be_send, axis, far)
    al1_send = al_keep[1] + al_in[1]
    be1_send = be_keep[1] + be_in[1]
    al1_in = swap(al1_send, axis, far)
    be1_in = swap(be1_send, axis, near)
    al1 = al_keep[0] + al_in[0]
    be1 = be_keep[0] + be_in[0]
    return al1 + al1_in, be1 + be1_in


def shards(queries, memory, w_query, w_key, w_value, w_out, grad_out, masked):
    seq = lax.axis_index("seq").astype(jnp.int32).reshape(1)
    head = lax.axis_index("head").astype(jnp.int32).reshape(1)
    keep_a, send_a, keep_b, send_b = run_main(
        seq, masked.reshape(32, 128), queries, grad_out, memory, w_query, w_key, w_value, w_out
    )
    in_a = swap(send_a, "seq", 1)
    in_b = swap(send_b, "seq", 1)

    def over_x(keep, got, cut):
        keep = keep.reshape(4, 2, *keep.shape[1:])
        got = got.reshape(4, 2, *got.shape[1:])
        pair = lambda i, j, lo, hi: jnp.stack(
            [keep[i, :, lo:hi] + got[i, :, lo:hi], keep[j, :, lo:hi] + got[j, :, lo:hi]]
        )
        top = keep.shape[2]
        return ring_reduce(
            pair(0, 3, 0, cut), pair(1, 2, 0, cut), pair(0, 1, cut, top), pair(3, 2, cut, top),
            "seq", 2, 6,
        )

    al, be = over_x(keep_a, in_a, 64)
    send = jnp.concatenate([al[1], be[1]], axis=0)
    got = swap(send, "seq", 8)
    mine = jnp.concatenate([al[0], be[0]], axis=0)
    keep_al, send_al, keep_be, send_be = run_head(head, mine, got, w_key, w_value)

    bl, bh = over_x(keep_b, in_b, 56)
    send = jnp.concatenate([bl[1], bh[1]], axis=0)
    b = jnp.concatenate([bl[0], bh[0]], axis=0) + swap(send, "seq", 8)
    total = b[96:97, 0:1]

    ml, mh = ring_reduce(keep_al, send_al, keep_be, send_be, "head", 1, 3)
    mem = jnp.concatenate([ml, mh], axis=1)
    grad_memory = (mem[0] + swap(mem[1], "head", 4)) / total

    b = b / total
    grad_wk = b[0:64, 0:64].T
    grad_wv = b[0:64, 64:128].T
    rest = b[64:96]
    grad_wq = jnp.concatenate([rest[:, 0:32], rest[:, 64:96]], axis=0).T
    grad_wo = jnp.concatenate([rest[:, 32:64], rest[:, 96:128]], axis=0)
    return (grad_wq, grad_wk, grad_wv, grad_wo, grad_memory)


def solution(mesh):
    return jax.shard_map(
        shards,
        mesh=mesh,
        in_specs=(
            P("seq", None),
            P(),
            P(None, "head"),
            P(None, "head"),
            P(None, "head"),
            P("head", None),
            P("seq", None),
            P("seq"),
        ),
        out_specs=(
            P("seq", "head"),
            P("seq", "head"),
            P("seq", "head"),
            P("head", "seq"),
            P("seq", "head"),
        ),
        check_vma=False,
    )
```

```python
import functools

import jax
import jax.numpy as jnp
from jax import lax
from jax.experimental import pallas as pl
from jax.experimental.pallas import tpu as pltpu
from jax.sharding import PartitionSpec as P

DH = 64
ROWS = 4096
LAT = 2048
E = 512
C = 1024
PACK = 256
SMALL = 128
LARGE = 272
TB = 256
MEM_PARTS = 4
ROW_PARTS = 4
f32 = jnp.float32
bf16 = jnp.bfloat16


def _dot(a, b, dims):
    return lax.dot_general(a, b, (dims, ((), ())), preferred_element_type=f32)


NN = ((1,), (0,))
NT = ((1,), (1,))


def main_kernel(
    sidx, masked, q_hbm, g_hbm, mem_hbm, wq_hbm, wk_hbm, wv_hbm, wo_hbm,
    keep_a, send_a, keep_b, send_b,
    q_in, g_in, mem, qc, gc, kv, wkv, wq2, wo2, pos, off_v, off_s,
    dkv, wqo, wkv_out, wqo_out,
    mem_sem, row_sem, w_sem, off_sem,
):
    me = sidx[0]
    w_copies = [
        pltpu.make_async_copy(src, dst, w_sem.at[i])
        for i, (src, dst) in enumerate(
            (
                (wk_hbm, wkv.at[pl.ds(0, DH)]),
                (wv_hbm, wkv.at[pl.ds(DH, DH)]),
                (wq_hbm, wq2.at[pl.ds(0, DH)]),
                (wo_hbm, wo2.at[pl.ds(DH, DH)]),
            )
        )
    ]
    mrows = LAT // MEM_PARTS
    mem_copies = [
        pltpu.make_async_copy(
            mem_hbm.at[pl.ds(i * mrows, mrows)], mem.at[pl.ds(i * mrows, mrows)], mem_sem.at[i]
        )
        for i in range(MEM_PARTS)
    ]
    rrows = ROWS // ROW_PARTS
    row_copies = [
        [
            pltpu.make_async_copy(
                src.at[pl.ds(i * rrows, rrows)], dst.at[pl.ds(i * rrows, rrows)], row_sem.at[2 * i + j]
            )
            for j, (src, dst) in enumerate(((q_hbm, q_in), (g_hbm, g_in)))
        ]
        for i in range(ROW_PARTS)
    ]
    for c in w_copies + mem_copies:
        c.start()
    for pair in row_copies:
        for c in pair:
            c.start()

    ones = masked[...].astype(f32)
    mb = ones.astype(bf16)
    r128 = lax.broadcasted_iota(jnp.int32, (128, 128), 0)
    c128 = lax.broadcasted_iota(jnp.int32, (128, 128), 1)
    before = (r128 < c128).astype(f32).astype(bf16)
    rank = _dot(mb, before, NN)
    counts = _dot(mb, jnp.ones((128, 128), bf16), NN)
    r40 = lax.broadcasted_iota(jnp.int32, (40, 32), 0)
    c40 = lax.broadcasted_iota(jnp.int32, (40, 32), 1)
    earlier = (c40 < r40).astype(f32).astype(bf16)
    offs = _dot(earlier, counts.astype(bf16), NN)
    off_v[...] = offs.astype(jnp.int32)
    off_copy = pltpu.make_async_copy(off_v, off_s, off_sem)
    off_copy.start()
    pos[...] = jnp.where(ones > 0.5, offs[:32] + rank, -1.0).astype(jnp.int32)

    dkv[...] = jnp.zeros_like(dkv)
    wqo[...] = jnp.zeros_like(wqo)
    qc[pl.ds(0, 16), :] = jnp.zeros((16, E), bf16)
    gc[pl.ds(0, 16), :] = jnp.zeros((16, E), bf16)

    for c in w_copies:
        c.wait()
    wq2[DH:, :] = jnp.zeros((DH, E), bf16)
    wo2[:DH, :] = jnp.zeros((DH, E), bf16)
    for i, c in enumerate(mem_copies):
        c.wait()
        part = pl.ds(i * mrows, mrows)
        kv[part, :] = _dot(mem[part, :], wkv[...], NT).astype(bf16)

    off_copy.wait()
    total = off_s[32, 0]

    def put(b, start, size):
        row = lax.broadcasted_iota(jnp.int32, (size, 128), 0) + start
        picks = [
            (row == pos[pl.ds(2 * b + half, 1), :]).astype(f32).astype(bf16) for half in range(2)
        ]
        pick = jnp.concatenate(picks, axis=1)
        src = pl.ds(b * PACK, PACK)
        first = pl.ds(start, 16)
        rest = pl.ds(pl.multiple_of(start + 16, 16), size - 16)
        for s_ref, d_ref in ((q_in, qc), (g_in, gc)):
            rows = _dot(pick, s_ref[src, :], NN)
            d_ref[first, :] = (rows[:16] + d_ref[first, :].astype(f32)).astype(bf16)
            d_ref[rest, :] = rows[16:].astype(bf16)

    per = rrows // PACK
    for b in range(ROWS // PACK):
        if b % per == 0:
            for c in row_copies[b // per]:
                c.wait()
        base = off_s[2 * b, 0]
        nxt = off_s[2 * b + 2, 0]
        start = pl.multiple_of((base // 16) * 16, 16)
        few = nxt - start < SMALL
        pl.when(few)(functools.partial(put, b, start, SMALL))
        pl.when(jnp.logical_not(few))(functools.partial(put, b, start, LARGE))

    tail = pl.ds(pl.multiple_of(((total + 15) // 16) * 16, 16), TB)
    qc[tail, :] = jnp.zeros((TB, E), bf16)
    gc[tail, :] = jnp.zeros((TB, E), bf16)

    def block(i, _):
        rows = pl.ds(pl.multiple_of(i * TB, TB), TB)
        q = qc[rows, :]
        g = gc[rows, :]
        qp = _dot(q, wq2[...], NT).astype(bf16).astype(f32) * 0.125
        da = _dot(g, wo2[...], NT).astype(bf16)
        score = _dot(qp.astype(bf16), kv[...], NT)
        dprob = _dot(da, kv[...], NT)
        top = jnp.max(score, axis=1, keepdims=True)
        e = jnp.exp(score - top)
        inv = 1.0 / jnp.sum(e, axis=1, keepdims=True)
        eb = e.astype(bf16)
        att = (_dot(eb, kv[...], NN) * inv).astype(bf16)
        daf = da.astype(f32)
        delta = jnp.sum(daf * att.astype(f32), axis=1, keepdims=True)
        ds = (e * (dprob - delta)).astype(bf16)
        dq = _dot(ds, kv[...], NN) * (inv * 0.125)
        lane = lax.broadcasted_iota(jnp.int32, (TB, 128), 1)
        x = jnp.where(lane < DH, dq, att.astype(f32))
        y = (qp + daf) * inv
        xt = x.T.astype(bf16)
        yt = y.T.astype(bf16)
        wqo[:DH, :] += _dot(xt[:DH], q, NN)
        wqo[DH:, :] += _dot(xt[DH:], g, NN)
        dkv[:DH, :] += _dot(yt[:DH], ds, NN)
        dkv[DH:, :] += _dot(yt[DH:], eb, NN)
        return 0

    lax.fori_loop(0, (total + TB - 1) // TB, block, 0)

    wkvt = _dot(dkv[...].astype(bf16), mem[...], NN)
    lane64 = lax.broadcasted_iota(jnp.int32, (64, 128), 1)
    for t in range(8):
        tk = wkvt[:DH, 128 * t : 128 * (t + 1)]
        tv = wkvt[DH:, 128 * t : 128 * (t + 1)]
        wkv_out[2 * t] = jnp.where(lane64 < DH, tk, pltpu.roll(tv, 64, 1))
        wkv_out[2 * t + 1] = jnp.where(lane64 < DH, pltpu.roll(tk, 64, 1), tv)
    lane32 = lax.broadcasted_iota(jnp.int32, (32, 128), 1)
    for t in range(4):
        cols = slice(128 * t, 128 * (t + 1))
        for u in range(4):
            chunk = None
            for k, lo in ((0, 0), (1, 64), (2, 32), (3, 96)):
                piece = wqo[lo : lo + 32, cols]
                shift = (32 * (k - u)) % 128
                piece = pltpu.roll(piece, shift, 1) if shift else piece
                chunk = piece if chunk is None else jnp.where(lane32 >= 32 * k, piece, chunk)
            wqo_out[4 * t + u] = chunk
    count = jnp.zeros((8, 128), f32) + total.astype(f32)
    for p in range(16):
        rc, rx, rz = p // 8, (p // 2) % 4, p % 2
        s = me ^ (rz * 8 + rx * 2 + rc)
        a = (keep_a, send_a)[rc]
        b = (keep_b, send_b)[rc]
        i = p % 8
        a[i] = dkv[:, pl.ds(pl.multiple_of(s * 128, 128), 128)]
        b[i, 0:64] = wkv_out[s]
        b[i, 64:96] = wqo_out[s]
        b[i, 96:104] = count


def run_main(sidx, masked, queries, grads, memory, w_query, w_key, w_value, w_out):
    any_ = pl.BlockSpec(memory_space=pl.ANY)
    vm = pl.BlockSpec(memory_space=pltpu.VMEM)
    a = jax.ShapeDtypeStruct((8, 128, 128), f32)
    b = jax.ShapeDtypeStruct((8, 104, 128), f32)
    pad = ROWS + LARGE + TB
    return pl.pallas_call(
        main_kernel,
        out_shape=(a, a, b, b),
        in_specs=[pl.BlockSpec(memory_space=pltpu.SMEM), vm] + [any_] * 7,
        out_specs=(vm,) * 4,
        scratch_shapes=[
            pltpu.VMEM((ROWS, E), bf16),
            pltpu.VMEM((ROWS, E), bf16),
            pltpu.VMEM((LAT, C), bf16),
            pltpu.VMEM((pad, E), bf16),
            pltpu.VMEM((pad, E), bf16),
            pltpu.VMEM((LAT, 128), bf16),
            pltpu.VMEM((128, C), bf16),
            pltpu.VMEM((128, E), bf16),
            pltpu.VMEM((128, E), bf16),
            pltpu.VMEM((32, 128), jnp.int32),
            pltpu.VMEM((40, 128), jnp.int32),
            pltpu.SMEM((40, 128), jnp.int32),
            pltpu.VMEM((128, LAT), f32),
            pltpu.VMEM((128, E), f32),
            pltpu.VMEM((16, 64, 128), f32),
            pltpu.VMEM((16, 32, 128), f32),
            pltpu.SemaphoreType.DMA((MEM_PARTS,)),
            pltpu.SemaphoreType.DMA((2 * ROW_PARTS,)),
            pltpu.SemaphoreType.DMA((4,)),
            pltpu.SemaphoreType.DMA(()),
        ],
        compiler_params=pltpu.CompilerParams(vmem_limit_bytes=48 * 1024 * 1024),
        cost_estimate=pl.CostEstimate(flops=10**10, bytes_accessed=14 * 2**20, transcendentals=10**7),
        name="masked_rows",
    )(sidx, masked, queries, grads, memory, w_query, w_key, w_value, w_out)


def head_kernel(hidx, part0, part1, wk, wv, keep_al, send_al, keep_be, send_be):
    me = hidx[0]
    dt = (part0[...] + part1[...]).T.astype(bf16)
    for ry in range(4):
        for rz in range(2):
            c = me ^ (rz * 4 + ry)
            cols = pl.ds(pl.multiple_of(c * 128, 128), 128)
            w = jnp.concatenate([wk[:, cols], wv[:, cols]], axis=0)
            out = _dot(dt, w, NN)
            al = (keep_al, 0) if ry == 0 else (keep_al, 1) if ry == 3 else (send_al, ry - 1)
            be = (keep_be, ry) if ry < 2 else (send_be, 3 - ry)
            al[0][al[1], rz] = out[:64]
            be[0][be[1], rz] = out[64:]


def run_head(hidx, part0, part1, wk_t, wv_t):
    vm = pl.BlockSpec(memory_space=pltpu.VMEM)
    o = jax.ShapeDtypeStruct((2, 2, 64, 128), f32)
    return pl.pallas_call(
        head_kernel,
        out_shape=(o,) * 4,
        in_specs=[pl.BlockSpec(memory_space=pltpu.SMEM)] + [vm] * 4,
        out_specs=(vm,) * 4,
        name="memory_part",
    )(hidx, part0, part1, wk_t, wv_t)


def weights_kernel(part0, part1, gwq, gwk, gwv, gwo_t, total):
    b = part0[...] + part1[...]
    count = b[96:104, :]
    total[...] = count
    b = b / count[0:1, :]
    kv_t = b[0:64].T
    gwk[...] = kv_t[:64]
    gwv[...] = kv_t[64:]
    qo_t = b[64:96].T
    gwq[...] = jnp.concatenate([qo_t[0:32], qo_t[64:96]], axis=1)
    gwo_t[...] = jnp.concatenate([qo_t[32:64], qo_t[96:128]], axis=1)


def run_weights(part0, part1):
    vm = pl.BlockSpec(memory_space=pltpu.VMEM)
    small = jax.ShapeDtypeStruct((32, 64), f32)
    square = jax.ShapeDtypeStruct((64, 64), f32)
    return pl.pallas_call(
        weights_kernel,
        out_shape=(small, square, square, small, jax.ShapeDtypeStruct((8, 128), f32)),
        in_specs=[vm] * 2,
        out_specs=(vm,) * 5,
        name="weight_parts",
    )(part0, part1)


def swap(x, axis, bits):
    n = lax.axis_size(axis)
    return lax.ppermute(x, axis, [(i, i ^ bits) for i in range(n)])


hold = lax.optimization_barrier


def shards(queries, memory, w_query, w_key, w_value, w_out, grad_out, masked):
    seq = lax.axis_index("seq").astype(jnp.int32).reshape(1)
    head = lax.axis_index("head").astype(jnp.int32).reshape(1)
    wk_t, wv_t = w_key.T, w_value.T
    keep_a, send_a, keep_b, send_b = run_main(
        seq, masked.reshape(32, 128), queries, grad_out, memory, w_query.T, wk_t, wv_t, w_out
    )
    got_a = swap(send_a, "seq", 1)
    sum_a = hold(keep_a + got_a).reshape(4, 2, 128, 128)
    al_send, be_send = sum_a[1:3, :, :64], jnp.stack([sum_a[3, :, 64:], sum_a[2, :, 64:]])
    al_send, be_send, send_b = hold((al_send, be_send, send_b))
    al_in = swap(al_send, "seq", 2)
    be_in = swap(be_send, "seq", 6)
    got_b = swap(send_b, "seq", 1)
    al_in, be_in, got_b = hold((al_in, be_in, got_b))

    al_send, be_send = hold((sum_a[3, :, :64] + al_in[1], sum_a[1, :, 64:] + be_in[1]))
    al_in2 = swap(al_send, "seq", 6)
    be_in2 = swap(be_send, "seq", 2)
    sum_b = hold(keep_b + got_b).reshape(4, 2, 104, 128)
    bl_send, bh_send = sum_b[1:3, :, :56], jnp.stack([sum_b[3, :, 56:], sum_b[2, :, 56:]])
    al = sum_a[0, :, :64] + al_in[0] + al_in2
    be = sum_a[0, :, 64:] + be_in[0] + be_in2
    sums = jnp.concatenate([al, be], axis=1)
    mine, send, bl_send, bh_send = hold((sums[0], sums[1], bl_send, bh_send))
    got = swap(send, "seq", 8)
    bl_in = swap(bl_send, "seq", 2)
    bh_in = swap(bh_send, "seq", 6)
    got, bl_in, bh_in = hold((got, bl_in, bh_in))

    keep_al, send_al, keep_be, send_be = run_head(head, mine, got, wk_t, wv_t)
    bl_send, bh_send = sum_b[3, :, :56] + bl_in[1], sum_b[1, :, 56:] + bh_in[1]
    send_al, send_be, bl_send, bh_send = hold((send_al, send_be, bl_send, bh_send))
    ml_in = swap(send_al, "head", 1)
    mh_in = swap(send_be, "head", 3)
    bl_in2 = swap(bl_send, "seq", 6)
    bh_in2 = swap(bh_send, "seq", 2)
    ml_in, mh_in, bl_in2, bh_in2 = hold((ml_in, mh_in, bl_in2, bh_in2))

    ml_send, mh_send = keep_al[1] + ml_in[1], keep_be[1] + mh_in[1]
    bl = sum_b[0, :, :56] + bl_in[0] + bl_in2
    bh = sum_b[0, :, 56:] + bh_in[0] + bh_in2
    sums = jnp.concatenate([bl, bh], axis=1)
    ml_send, mh_send, mine_b, send_b = hold((ml_send, mh_send, sums[0], sums[1]))
    ml_in2 = swap(ml_send, "head", 3)
    mh_in2 = swap(mh_send, "head", 1)
    got_b = swap(send_b, "seq", 8)
    ml_in2, mh_in2, got_b = hold((ml_in2, mh_in2, got_b))

    ml = keep_al[0] + ml_in[0] + ml_in2
    mh = keep_be[0] + mh_in[0] + mh_in2
    mem = jnp.concatenate([ml, mh], axis=1)
    mine, send = hold((mem[0], mem[1]))
    got = swap(send, "head", 4)
    grad_wq, grad_wk, grad_wv, grad_wo_t, total = run_weights(mine_b, got_b)
    grad_memory = (mine + got) / total[0:1, :]
    return (grad_wq, grad_wk, grad_wv, grad_wo_t.T, grad_memory)


def solution(mesh):
    return jax.shard_map(
        shards,
        mesh=mesh,
        in_specs=(
            P("seq", None),
            P(),
            P(None, "head"),
            P(None, "head"),
            P(None, "head"),
            P("head", None),
            P("seq", None),
            P("seq"),
        ),
        out_specs=(
            P("seq", "head"),
            P("seq", "head"),
            P("seq", "head"),
            P("head", "seq"),
            P("seq", "head"),
        ),
        check_vma=False,
    )
```

```python
import functools

import jax
import jax.numpy as jnp
from jax import lax
from jax.experimental import pallas as pl
from jax.experimental.pallas import tpu as pltpu
from jax.sharding import PartitionSpec as P

DH = 64
ROWS = 4096
LAT = 2048
E = 512
C = 1024
PACK = 256
SMALL = 128
LARGE = 272
TB = 256
MEM_PARTS = 4
ROW_PARTS = 4
f32 = jnp.float32
bf16 = jnp.bfloat16


def _dot(a, b, dims):
    return lax.dot_general(a, b, (dims, ((), ())), preferred_element_type=f32)


NN = ((1,), (0,))
NT = ((1,), (1,))


def main_kernel(
    sidx, masked_hbm, q_hbm, g_hbm, mem_hbm, wq_hbm, wk_hbm, wv_hbm, wo_hbm,
    keep_a, send_a, keep_b, send_b,
    masked, q_in, g_in, mem, qc, gc, kv, wkv, wq2, wo2, pos, off_v, off_s,
    dkv, wqo, wkv_out, wqo_out,
    mem_sem, row_sem, w_sem, off_sem,
):
    me = sidx[0]
    w_copies = [
        pltpu.make_async_copy(src, dst, w_sem.at[i])
        for i, (src, dst) in enumerate(
            (
                (wk_hbm, wkv.at[pl.ds(0, DH)]),
                (wv_hbm, wkv.at[pl.ds(DH, DH)]),
                (wq_hbm, wq2.at[pl.ds(0, DH)]),
                (wo_hbm, wo2.at[pl.ds(DH, DH)]),
            )
        )
    ]
    mrows = LAT // MEM_PARTS
    mem_copies = [
        pltpu.make_async_copy(
            mem_hbm.at[pl.ds(i * mrows, mrows)], mem.at[pl.ds(i * mrows, mrows)], mem_sem.at[i]
        )
        for i in range(MEM_PARTS)
    ]
    rrows = ROWS // ROW_PARTS
    row_copies = [
        [
            pltpu.make_async_copy(
                src.at[pl.ds(i * rrows, rrows)], dst.at[pl.ds(i * rrows, rrows)], row_sem.at[2 * i + j]
            )
            for j, (src, dst) in enumerate(((q_hbm, q_in), (g_hbm, g_in)))
        ]
        for i in range(ROW_PARTS)
    ]
    mask_copy = pltpu.make_async_copy(masked_hbm, masked, off_sem)
    mask_copy.start()
    for c in w_copies + mem_copies:
        c.start()
    for pair in row_copies:
        for c in pair:
            c.start()

    mask_copy.wait()
    ones = masked[...].astype(f32)
    mb = ones.astype(bf16)
    r128 = lax.broadcasted_iota(jnp.int32, (128, 128), 0)
    c128 = lax.broadcasted_iota(jnp.int32, (128, 128), 1)
    before = (r128 < c128).astype(f32).astype(bf16)
    rank = _dot(mb, before, NN)
    counts = _dot(mb, jnp.ones((128, 128), bf16), NN)
    r40 = lax.broadcasted_iota(jnp.int32, (40, 32), 0)
    c40 = lax.broadcasted_iota(jnp.int32, (40, 32), 1)
    earlier = (c40 < r40).astype(f32).astype(bf16)
    offs = _dot(earlier, counts.astype(bf16), NN)
    off_v[...] = offs.astype(jnp.int32)
    off_copy = pltpu.make_async_copy(off_v, off_s, off_sem)
    off_copy.start()
    pos[...] = jnp.where(ones > 0.5, offs[:32] + rank, -1.0).astype(jnp.int32)

    dkv[...] = jnp.zeros_like(dkv)
    wqo[...] = jnp.zeros_like(wqo)
    qc[pl.ds(0, 16), :] = jnp.zeros((16, E), bf16)
    gc[pl.ds(0, 16), :] = jnp.zeros((16, E), bf16)

    for c in w_copies:
        c.wait()
    wq2[DH:, :] = jnp.zeros((DH, E), bf16)
    wo2[:DH, :] = jnp.zeros((DH, E), bf16)
    for i, c in enumerate(mem_copies):
        c.wait()
        part = pl.ds(i * mrows, mrows)
        kv[part, :] = _dot(mem[part, :], wkv[...], NT).astype(bf16)

    off_copy.wait()
    total = off_s[32, 0]

    def put(b, start, size):
        row = lax.broadcasted_iota(jnp.int32, (size, 128), 0) + start
        picks = [
            (row == pos[pl.ds(2 * b + half, 1), :]).astype(f32).astype(bf16) for half in range(2)
        ]
        pick = jnp.concatenate(picks, axis=1)
        src = pl.ds(b * PACK, PACK)
        first = pl.ds(start, 16)
        rest = pl.ds(pl.multiple_of(start + 16, 16), size - 16)
        for s_ref, d_ref in ((q_in, qc), (g_in, gc)):
            rows = _dot(pick, s_ref[src, :], NN)
            d_ref[first, :] = (rows[:16] + d_ref[first, :].astype(f32)).astype(bf16)
            d_ref[rest, :] = rows[16:].astype(bf16)

    per = rrows // PACK
    for b in range(ROWS // PACK):
        if b % per == 0:
            for c in row_copies[b // per]:
                c.wait()
        base = off_s[2 * b, 0]
        nxt = off_s[2 * b + 2, 0]
        start = pl.multiple_of((base // 16) * 16, 16)
        few = nxt - start < SMALL
        pl.when(few)(functools.partial(put, b, start, SMALL))
        pl.when(jnp.logical_not(few))(functools.partial(put, b, start, LARGE))

    tail = pl.ds(pl.multiple_of(((total + 15) // 16) * 16, 16), TB)
    qc[tail, :] = jnp.zeros((TB, E), bf16)
    gc[tail, :] = jnp.zeros((TB, E), bf16)

    def block(i, _):
        rows = pl.ds(pl.multiple_of(i * TB, TB), TB)
        q = qc[rows, :]
        g = gc[rows, :]
        qp = _dot(q, wq2[...], NT).astype(bf16).astype(f32) * 0.125
        da = _dot(g, wo2[...], NT).astype(bf16)
        score = _dot(qp.astype(bf16), kv[...], NT)
        dprob = _dot(da, kv[...], NT)
        top = jnp.max(score, axis=1, keepdims=True)
        e = jnp.exp(score - top)
        inv = 1.0 / jnp.sum(e, axis=1, keepdims=True)
        eb = e.astype(bf16)
        att = (_dot(eb, kv[...], NN) * inv).astype(bf16)
        daf = da.astype(f32)
        delta = jnp.sum(daf * att.astype(f32), axis=1, keepdims=True)
        ds = (e * (dprob - delta)).astype(bf16)
        dq = _dot(ds, kv[...], NN) * (inv * 0.125)
        lane = lax.broadcasted_iota(jnp.int32, (TB, 128), 1)
        x = jnp.where(lane < DH, dq, att.astype(f32))
        y = (qp + daf) * inv
        xt = x.T.astype(bf16)
        yt = y.T.astype(bf16)
        wqo[:DH, :] += _dot(xt[:DH], q, NN)
        wqo[DH:, :] += _dot(xt[DH:], g, NN)
        dkv[:DH, :] += _dot(yt[:DH], ds, NN)
        dkv[DH:, :] += _dot(yt[DH:], eb, NN)
        return 0

    lax.fori_loop(0, (total + TB - 1) // TB, block, 0)

    wkvt = _dot(dkv[...].astype(bf16), mem[...], NN)
    lane64 = lax.broadcasted_iota(jnp.int32, (64, 128), 1)
    for t in range(8):
        tk = wkvt[:DH, 128 * t : 128 * (t + 1)]
        tv = wkvt[DH:, 128 * t : 128 * (t + 1)]
        wkv_out[2 * t] = jnp.where(lane64 < DH, tk, pltpu.roll(tv, 64, 1))
        wkv_out[2 * t + 1] = jnp.where(lane64 < DH, pltpu.roll(tk, 64, 1), tv)
    lane32 = lax.broadcasted_iota(jnp.int32, (32, 128), 1)
    for t in range(4):
        cols = slice(128 * t, 128 * (t + 1))
        for u in range(4):
            chunk = None
            for k, lo in ((0, 0), (1, 64), (2, 32), (3, 96)):
                piece = wqo[lo : lo + 32, cols]
                shift = (32 * (k - u)) % 128
                piece = pltpu.roll(piece, shift, 1) if shift else piece
                chunk = piece if chunk is None else jnp.where(lane32 >= 32 * k, piece, chunk)
            wqo_out[4 * t + u] = chunk
    count = jnp.zeros((8, 128), f32) + total.astype(f32)
    core = me & 1
    for p in range(16):
        i, rc = p % 8, p // 8
        z, x = i // 4, i % 4
        a = (keep_a, send_a)[rc]
        b = (keep_b, send_b)[rc]
        s = z * 8 + x * 2 + (core ^ rc)
        a[i] = dkv[:, pl.ds(pl.multiple_of(s * 128, 128), 128)]
        s = me ^ (z * 8 + x * 2 + rc)
        b[i, 0:64] = wkv_out[s]
        b[i, 64:96] = wqo_out[s]
        b[i, 96:104] = count


def in_hbm(x):
    return pltpu.with_memory_space_constraint(x, pltpu.HBM)


def in_vmem(x):
    return pltpu.with_memory_space_constraint(x, pltpu.VMEM)


def run_main(sidx, masked, queries, grads, memory, w_query, w_key, w_value, w_out):
    any_ = pl.BlockSpec(memory_space=pl.ANY)
    vm = pl.BlockSpec(memory_space=pltpu.VMEM)
    a = pltpu.VMEM((8, 128, 128), f32)
    b = pltpu.VMEM((8, 104, 128), f32)
    arrays = [in_hbm(x) for x in (queries, grads, memory, w_query, w_key, w_value, w_out)]
    pad = ROWS + LARGE + TB
    return pl.pallas_call(
        main_kernel,
        out_shape=(a, a, b, b),
        in_specs=[pl.BlockSpec(memory_space=pltpu.SMEM)] + [any_] * 8,
        out_specs=(vm,) * 4,
        scratch_shapes=[
            pltpu.VMEM((32, 128), jnp.int32),
            pltpu.VMEM((ROWS, E), bf16),
            pltpu.VMEM((ROWS, E), bf16),
            pltpu.VMEM((LAT, C), bf16),
            pltpu.VMEM((pad, E), bf16),
            pltpu.VMEM((pad, E), bf16),
            pltpu.VMEM((LAT, 128), bf16),
            pltpu.VMEM((128, C), bf16),
            pltpu.VMEM((128, E), bf16),
            pltpu.VMEM((128, E), bf16),
            pltpu.VMEM((32, 128), jnp.int32),
            pltpu.VMEM((40, 128), jnp.int32),
            pltpu.SMEM((40, 128), jnp.int32),
            pltpu.VMEM((128, LAT), f32),
            pltpu.VMEM((128, E), f32),
            pltpu.VMEM((16, 64, 128), f32),
            pltpu.VMEM((16, 32, 128), f32),
            pltpu.SemaphoreType.DMA((MEM_PARTS,)),
            pltpu.SemaphoreType.DMA((2 * ROW_PARTS,)),
            pltpu.SemaphoreType.DMA((4,)),
            pltpu.SemaphoreType.DMA(()),
        ],
        compiler_params=pltpu.CompilerParams(vmem_limit_bytes=48 * 1024 * 1024),
        cost_estimate=pl.CostEstimate(flops=10**10, bytes_accessed=14 * 2**20, transcendentals=10**7),
        name="masked_rows",
    )(sidx, in_hbm(masked), *arrays)


def head_kernel(parts, wk, wv, out):
    d = parts[0]
    for k in range(1, 8):
        d = d + parts[k]
    dt = d.T.astype(bf16)
    for c in range(8):
        cols = slice(128 * c, 128 * (c + 1))
        w = jnp.concatenate([wk[:, cols], wv[:, cols]], axis=0)
        out[c] = _dot(dt, w, NN)


def run_head(parts, wk_t, wv_t):
    vm = pl.BlockSpec(memory_space=pltpu.VMEM)
    return pl.pallas_call(
        head_kernel,
        out_shape=pltpu.VMEM((8, 128, 128), f32),
        in_specs=[vm] * 3,
        out_specs=vm,
        name="memory_part",
    )(in_vmem(parts), in_vmem(wk_t), in_vmem(wv_t))


def last_kernel(mine, got, parts, gwq, gwk, gwv, gwo_t, gmem):
    b = mine[...] + got[...]
    scale = 1.0 / b[96:97, :]
    b = b * scale
    kv_t = b[0:64].T
    gwk[...] = kv_t[:64]
    gwv[...] = kv_t[64:]
    qo_t = b[64:96].T
    gwq[...] = jnp.concatenate([qo_t[0:32], qo_t[64:96]], axis=1)
    gwo_t[...] = jnp.concatenate([qo_t[32:64], qo_t[96:128]], axis=1)
    m = parts[0]
    for k in range(1, 8):
        m = m + parts[k]
    gmem[...] = m * scale


def run_last(mine, got, parts):
    vm = pl.BlockSpec(memory_space=pltpu.VMEM)
    small = jax.ShapeDtypeStruct((32, 64), f32)
    square = jax.ShapeDtypeStruct((64, 64), f32)
    return pl.pallas_call(
        last_kernel,
        out_shape=(small, square, square, small, jax.ShapeDtypeStruct((128, 128), f32)),
        in_specs=[vm] * 3,
        out_specs=(vm,) * 5,
        name="gradients",
    )(in_vmem(mine), in_vmem(got), in_vmem(parts))


def swap(x, axis, bits):
    n = lax.axis_size(axis)
    return lax.ppermute(x, axis, [(i, i ^ bits) for i in range(n)])


hold = lax.optimization_barrier


def shards(queries, memory, w_query, w_key, w_value, w_out, grad_out, masked):
    seq = lax.axis_index("seq").astype(jnp.int32).reshape(1)
    wk_t, wv_t = w_key.T, w_value.T
    keep_a, send_a, keep_b, send_b = run_main(
        seq, masked.reshape(32, 128), queries, grad_out, memory, w_query.T, wk_t, wv_t, w_out
    )
    got_a = swap(send_a, "seq", 1)
    got_b = swap(send_b, "seq", 1)
    groups = [[z * 8 + x * 2 + core for z in range(2) for x in range(4)] for core in range(2)]
    sum_a, sum_b = hold((keep_a + got_a, keep_b + got_b))
    sum_b = sum_b.reshape(2, 4, 104, 128)
    sends = hold((sum_b[:, 1], sum_b[:, 3], sum_b[:, 2]))
    ins = [swap(x, "seq", bits) for x, bits in zip(sends, (2, 6, 4))]
    parts = lax.all_to_all(sum_a, "seq", 0, 0, axis_index_groups=groups)
    parts, ins = hold((parts, ins))
    part = run_head(parts, wk_t, wv_t)

    sum_b = sum_b[:, 0] + ins[0] + ins[1] + ins[2]
    part, mine, send = hold((part, sum_b[0], sum_b[1]))
    got = swap(send, "seq", 8)
    parts = lax.all_to_all(part, "head", 0, 0)
    grad_wq, grad_wk, grad_wv, grad_wo_t, grad_memory = run_last(mine, got, parts)
    return (grad_wq, grad_wk, grad_wv, grad_wo_t.T, grad_memory)


def solution(mesh):
    return jax.shard_map(
        shards,
        mesh=mesh,
        in_specs=(
            P("seq", None),
            P(),
            P(None, "head"),
            P(None, "head"),
            P(None, "head"),
            P("head", None),
            P("seq", None),
            P("seq"),
        ),
        out_specs=(
            P("seq", "head"),
            P("seq", "head"),
            P("seq", "head"),
            P("head", "seq"),
            P("seq", "head"),
        ),
        check_vma=False,
    )
```

```python
import functools

import jax
import jax.numpy as jnp
from jax import lax
from jax.experimental import pallas as pl
from jax.experimental.pallas import tpu as pltpu
from jax.sharding import PartitionSpec as P

DH = 64
ROWS = 4096
LAT = 2048
E = 512
C = 1024
PACK = 256
SMALL = 128
LARGE = 272
TB = 256
CH = 512
ROW_PARTS = 2
MEM_PARTS = 2
AHEAD = 1
CHUNK = 128 + 64 + 32 + 8
f32 = jnp.float32
bf16 = jnp.bfloat16


def _dot(a, b, dims):
    return lax.dot_general(a, b, (dims, ((), ())), preferred_element_type=f32)


NN = ((1,), (0,))
NT = ((1,), (1,))


def main_kernel(
    sidx, masked_hbm, q_hbm, g_hbm, mem_hbm, wq_hbm, wk_hbm, wv_hbm, wo_hbm,
    keep, send,
    masked, q_in, g_in, mem, qc, gc, kv, wkv, wq2, wo2, pos, off_v, off_s,
    kvt, sc_s, dp_s, eb_s,
    dkv, wqo, wkv_out, wqo_out,
    mem_sem, row_sem, w_sem, off_sem,
):
    me = sidx[0]
    w_copies = [
        pltpu.make_async_copy(src, dst, w_sem.at[i])
        for i, (src, dst) in enumerate(
            (
                (wk_hbm, wkv.at[pl.ds(0, DH)]),
                (wv_hbm, wkv.at[pl.ds(DH, DH)]),
                (wq_hbm, wq2.at[pl.ds(0, DH)]),
                (wo_hbm, wo2.at[pl.ds(DH, DH)]),
            )
        )
    ]
    mrows = LAT // MEM_PARTS
    mem_parts = [pl.ds(i * mrows, mrows) for i in range(MEM_PARTS)]
    mem_copies = [
        pltpu.make_async_copy(mem_hbm.at[part], mem.at[part], mem_sem.at[i])
        for i, part in enumerate(mem_parts)
    ]
    rrows = ROWS // ROW_PARTS
    row_copies = [
        [
            pltpu.make_async_copy(
                src.at[pl.ds(i * rrows, rrows)], dst.at[pl.ds(i * rrows, rrows)], row_sem.at[2 * i + j]
            )
            for j, (src, dst) in enumerate(((q_hbm, q_in), (g_hbm, g_in)))
        ]
        for i in range(ROW_PARTS)
    ]
    mask_copy = pltpu.make_async_copy(masked_hbm, masked, off_sem)
    mask_copy.start()
    for pair in row_copies[:AHEAD]:
        for c in pair:
            c.start()

    mask_copy.wait()
    ones = masked[...].astype(f32)
    mb = ones.astype(bf16)
    r128 = lax.broadcasted_iota(jnp.int32, (128, 128), 0)
    c128 = lax.broadcasted_iota(jnp.int32, (128, 128), 1)
    before = (r128 < c128).astype(f32).astype(bf16)
    rank = _dot(mb, before, NN)
    counts = _dot(mb, jnp.ones((128, 128), bf16), NN)
    r40 = lax.broadcasted_iota(jnp.int32, (40, 32), 0)
    c40 = lax.broadcasted_iota(jnp.int32, (40, 32), 1)
    earlier = (c40 < r40).astype(f32).astype(bf16)
    offs = _dot(earlier, counts.astype(bf16), NN)
    off_v[...] = offs.astype(jnp.int32)
    off_copy = pltpu.make_async_copy(off_v, off_s, off_sem)
    off_copy.start()
    pos[...] = jnp.where(ones > 0.5, offs[:32] + rank, -1.0).astype(jnp.int32)

    dkv[...] = jnp.zeros_like(dkv)
    wqo[...] = jnp.zeros_like(wqo)
    qc[pl.ds(0, 16), :] = jnp.zeros((16, E), bf16)
    gc[pl.ds(0, 16), :] = jnp.zeros((16, E), bf16)

    wq2[DH:, :] = jnp.zeros((DH, E), bf16)
    wo2[:DH, :] = jnp.zeros((DH, E), bf16)
    off_copy.wait()
    total = off_s[32, 0]

    def put(b, start, size):
        row = lax.broadcasted_iota(jnp.int32, (size, 128), 0) + start
        picks = [
            (row == pos[pl.ds(2 * b + half, 1), :]).astype(f32).astype(bf16) for half in range(2)
        ]
        pick = jnp.concatenate(picks, axis=1)
        src = pl.ds(b * PACK, PACK)
        first = pl.ds(start, 16)
        rest = pl.ds(pl.multiple_of(start + 16, 16), size - 16)
        for s_ref, d_ref in ((q_in, qc), (g_in, gc)):
            rows = _dot(pick, s_ref[src, :], NN)
            d_ref[first, :] = (rows[:16] + d_ref[first, :].astype(f32)).astype(bf16)
            d_ref[rest, :] = rows[16:].astype(bf16)

    per = rrows // PACK
    for b in range(ROWS // PACK):
        if b % per == 0:
            part = b // per
            for c in row_copies[part]:
                c.wait()
            for c in row_copies[part + AHEAD] if part + AHEAD < ROW_PARTS else ():
                c.start()
            if part + AHEAD == ROW_PARTS:
                for c in w_copies + mem_copies:
                    c.start()
        base = off_s[2 * b, 0]
        nxt = off_s[2 * b + 2, 0]
        start = pl.multiple_of((base // 16) * 16, 16)
        few = nxt - start < SMALL
        pl.when(few)(functools.partial(put, b, start, SMALL))
        pl.when(jnp.logical_not(few))(functools.partial(put, b, start, LARGE))

    for c in w_copies:
        c.wait()
    for c, part in zip(mem_copies, mem_parts):
        c.wait()
        proj = _dot(mem[part, :], wkv[...], NT)
        kv[part, :] = proj.astype(bf16)
        kvt[:, part] = proj.T.astype(bf16)

    tail = pl.ds(pl.multiple_of(((total + 15) // 16) * 16, 16), TB)
    qc[tail, :] = jnp.zeros((TB, E), bf16)
    gc[tail, :] = jnp.zeros((TB, E), bf16)

    half = lax.broadcasted_iota(jnp.int32, (TB, 128), 1) < DH
    none = jnp.zeros((DH, TB), bf16)
    parts = [slice(c * CH, (c + 1) * CH) for c in range(LAT // CH)]

    def fold(x, op):
        rows = [x[8 * k : 8 * (k + 1)] for k in range(x.shape[0] // 8)]
        while len(rows) > 1:
            rows = [op(a, b) for a, b in zip(rows[::2], rows[1::2])]
        return rows[0]

    def begin(i):
        rows = pl.ds(pl.multiple_of(i * TB, TB), TB)
        qp = _dot(qc[rows, :], wq2[...], NT).astype(bf16).astype(f32) * 0.125
        da = _dot(gc[rows, :], wo2[...], NT).astype(bf16).astype(f32)
        zt = (qp + da).T
        qt = jnp.concatenate([zt[:DH].astype(bf16), none], axis=0)
        gt = jnp.concatenate([none, zt[DH:].astype(bf16)], axis=0)
        return zt, qt, gt

    def scores(qt, part):
        score = _dot(kv[part, :], qt, NN)
        sc_s[part, :] = score
        return fold(score, jnp.maximum)

    def over(op, a, b):
        return b if a is None else op(a, b)

    zt0, qt0, gt0 = begin(0)
    top0 = None
    for part in parts:
        top0 = over(jnp.maximum, top0, scores(qt0, part))
        dp_s[part, :] = _dot(kv[part, :], gt0, NN)

    def block(i, carried):
        zt, top = carried
        zt_n, qt_n, gt_n = begin(i + 1)
        top = jnp.max(top, axis=0, keepdims=True)
        norm = att = dq = top_n = None
        for part in parts:
            e = jnp.exp(sc_s[part, :] - top)
            eb = e.astype(bf16)
            eb_s[part, :] = eb
            norm = over(jnp.add, norm, fold(e, jnp.add))
            att = over(jnp.add, att, _dot(kvt[DH:, part], eb, NN))
            top_n = over(jnp.maximum, top_n, scores(qt_n, part))
        inv = 1.0 / jnp.sum(norm, axis=0, keepdims=True)
        att = (att * inv).astype(bf16).astype(f32)
        delta = jnp.sum(zt[DH:] * att, axis=0, keepdims=True)
        y = (zt * inv).T
        yk = jnp.where(half, y, 0.0).astype(bf16)
        yv = jnp.where(half, 0.0, y).astype(bf16)
        for part in parts:
            eb = eb_s[part, :]
            ds = (eb.astype(f32) * (dp_s[part, :] - delta)).astype(bf16)
            dp_s[part, :] = _dot(kv[part, :], gt_n, NN)
            dq = over(jnp.add, dq, _dot(kvt[:DH, part], ds, NN))
            dkv[part, :] += _dot(ds, yk, NN) + _dot(eb, yv, NN)
        rows = pl.ds(pl.multiple_of(i * TB, TB), TB)
        xq = (dq * (inv * 0.125)).astype(bf16)
        wqo[:DH, :] += _dot(xq, qc[rows, :], NN)
        wqo[DH:, :] += _dot(att.astype(bf16), gc[rows, :], NN)
        return zt_n, top_n

    lax.fori_loop(0, (total + TB - 1) // TB, block, (zt0, top0))

    wkvt = _dot(dkv[...].T.astype(bf16), mem[...], NN)
    lane64 = lax.broadcasted_iota(jnp.int32, (64, 128), 1)
    for t in range(8):
        tk = wkvt[:DH, 128 * t : 128 * (t + 1)]
        tv = wkvt[DH:, 128 * t : 128 * (t + 1)]
        wkv_out[2 * t] = jnp.where(lane64 < DH, tk, pltpu.roll(tv, 64, 1))
        wkv_out[2 * t + 1] = jnp.where(lane64 < DH, pltpu.roll(tk, 64, 1), tv)
    lane32 = lax.broadcasted_iota(jnp.int32, (32, 128), 1)
    for t in range(4):
        cols = slice(128 * t, 128 * (t + 1))
        for u in range(4):
            chunk = None
            for k, lo in ((0, 0), (1, 64), (2, 32), (3, 96)):
                piece = wqo[lo : lo + 32, cols]
                shift = (32 * (k - u)) % 128
                piece = pltpu.roll(piece, shift, 1) if shift else piece
                chunk = piece if chunk is None else jnp.where(lane32 >= 32 * k, piece, chunk)
            wqo_out[4 * t + u] = chunk
    count = jnp.zeros((8, 128), f32) + total.astype(f32)
    core = me & 1
    for p in range(16):
        i, rc = p % 8, p // 8
        out = (keep, send)[rc]
        s = (i // 4) * 8 + (i % 4) * 2 + (core ^ rc)
        out[i, 0:128] = dkv[pl.ds(pl.multiple_of(s * 128, 128), 128), :]
        out[i, 128:192] = wkv_out[s]
        out[i, 192:224] = wqo_out[s]
        out[i, 224:232] = count


def in_hbm(x):
    return pltpu.with_memory_space_constraint(x, pltpu.HBM)


def in_vmem(x):
    return pltpu.with_memory_space_constraint(x, pltpu.VMEM)


def run_main(sidx, masked, queries, grads, memory, w_query, w_key, w_value, w_out):
    any_ = pl.BlockSpec(memory_space=pl.ANY)
    vm = pl.BlockSpec(memory_space=pltpu.VMEM)
    a = pltpu.VMEM((8, CHUNK, 128), f32)
    arrays = [in_hbm(x) for x in (queries, grads, memory, w_query, w_key, w_value, w_out)]
    pad = ROWS + LARGE + TB
    return pl.pallas_call(
        main_kernel,
        out_shape=(a, a),
        in_specs=[pl.BlockSpec(memory_space=pltpu.SMEM)] + [any_] * 8,
        out_specs=(vm,) * 2,
        scratch_shapes=[
            pltpu.VMEM((32, 128), jnp.int32),
            pltpu.VMEM((ROWS, E), bf16),
            pltpu.VMEM((ROWS, E), bf16),
            pltpu.VMEM((LAT, C), bf16),
            pltpu.VMEM((pad, E), bf16),
            pltpu.VMEM((pad, E), bf16),
            pltpu.VMEM((LAT, 128), bf16),
            pltpu.VMEM((128, C), bf16),
            pltpu.VMEM((128, E), bf16),
            pltpu.VMEM((128, E), bf16),
            pltpu.VMEM((32, 128), jnp.int32),
            pltpu.VMEM((40, 128), jnp.int32),
            pltpu.SMEM((40, 128), jnp.int32),
            pltpu.VMEM((128, LAT), bf16),
            pltpu.VMEM((LAT, TB), f32),
            pltpu.VMEM((LAT, TB), f32),
            pltpu.VMEM((LAT, TB), bf16),
            pltpu.VMEM((LAT, 128), f32),
            pltpu.VMEM((128, E), f32),
            pltpu.VMEM((16, 64, 128), f32),
            pltpu.VMEM((16, 32, 128), f32),
            pltpu.SemaphoreType.DMA((MEM_PARTS,)),
            pltpu.SemaphoreType.DMA((2 * ROW_PARTS,)),
            pltpu.SemaphoreType.DMA((4,)),
            pltpu.SemaphoreType.DMA(()),
        ],
        compiler_params=pltpu.CompilerParams(vmem_limit_bytes=48 * 1024 * 1024),
        cost_estimate=pl.CostEstimate(flops=10**10, bytes_accessed=14 * 2**20, transcendentals=10**7),
        name="masked_rows",
    )(sidx, in_hbm(masked), *arrays)


VM = pl.BlockSpec(memory_space=pltpu.VMEM)


def total_of(parts, rows):
    t = parts[0, rows]
    for k in range(1, parts.shape[0]):
        t = t + parts[k, rows]
    return t


def head_kernel(parts, wk, wv, out, rest):
    dt = total_of(parts, slice(0, 128)).astype(bf16)
    for c in range(8):
        cols = slice(128 * c, 128 * (c + 1))
        w = jnp.concatenate([wk[:, cols], wv[:, cols]], axis=0)
        out[c] = _dot(dt, w, NN)
    rest[...] = total_of(parts, slice(128, CHUNK))


def run_head(parts, wk_t, wv_t):
    return pl.pallas_call(
        head_kernel,
        out_shape=(pltpu.VMEM((8, 128, 128), f32), pltpu.VMEM((CHUNK - 128, 128), f32)),
        in_specs=[VM] * 3,
        out_specs=(VM,) * 2,
        name="memory_part",
    )(in_vmem(parts), in_vmem(wk_t), in_vmem(wv_t))


def weights_kernel(rest, gwq, gwk, gwv, gwo_t, scale_out):
    scale = 1.0 / rest[96:104, :]
    scale_out[...] = scale
    b = rest[0:96] * scale[0:1]
    kv_t = b[0:64].T
    gwk[...] = kv_t[:64]
    gwv[...] = kv_t[64:]
    qo_t = b[64:96].T
    gwq[...] = jnp.concatenate([qo_t[0:32], qo_t[64:96]], axis=1)
    gwo_t[...] = jnp.concatenate([qo_t[32:64], qo_t[96:128]], axis=1)


def run_weights(rest):
    small = jax.ShapeDtypeStruct((32, 64), f32)
    square = jax.ShapeDtypeStruct((64, 64), f32)
    return pl.pallas_call(
        weights_kernel,
        out_shape=(small, square, square, small, pltpu.VMEM((8, 128), f32)),
        in_specs=[VM],
        out_specs=(VM,) * 5,
        name="weight_parts",
    )(in_vmem(rest))


def last_kernel(parts, scale, gmem):
    gmem[...] = total_of(parts, slice(0, 128)) * scale[0:1]


def run_last(parts, scale):
    return pl.pallas_call(
        last_kernel,
        out_shape=jax.ShapeDtypeStruct((128, 128), f32),
        in_specs=[VM] * 2,
        out_specs=VM,
        name="grad_memory",
    )(in_vmem(parts), in_vmem(scale))


def swap(x, axis, bits):
    n = lax.axis_size(axis)
    return lax.ppermute(x, axis, [(i, i ^ bits) for i in range(n)])


def shards(queries, memory, w_query, w_key, w_value, w_out, grad_out, masked):
    seq = lax.axis_index("seq").astype(jnp.int32).reshape(1)
    wk_t, wv_t = w_key.T, w_value.T
    keep, send = run_main(
        seq, masked.reshape(32, 128), queries, grad_out, memory, w_query.T, wk_t, wv_t, w_out
    )
    groups = [[z * 8 + x * 2 + core for z in range(2) for x in range(4)] for core in range(2)]
    parts = lax.all_to_all(keep + swap(send, "seq", 1), "seq", 0, 0, axis_index_groups=groups)
    part, rest = run_head(parts, wk_t, wv_t)
    grad_wq, grad_wk, grad_wv, grad_wo_t, scale = run_weights(rest)
    grad_memory = run_last(lax.all_to_all(part, "head", 0, 0), scale)
    return (grad_wq, grad_wk, grad_wv, grad_wo_t.T, grad_memory)


def solution(mesh):
    return jax.shard_map(
        shards,
        mesh=mesh,
        in_specs=(
            P("seq", None),
            P(),
            P(None, "head"),
            P(None, "head"),
            P(None, "head"),
            P("head", None),
            P("seq", None),
            P("seq"),
        ),
        out_specs=(
            P("seq", "head"),
            P("seq", "head"),
            P("seq", "head"),
            P("head", "seq"),
            P("seq", "head"),
        ),
        check_vma=False,
    )
```

```python
import functools

import jax
import jax.numpy as jnp
from jax import lax
from jax.experimental import pallas as pl
from jax.experimental.pallas import tpu as pltpu
from jax.sharding import PartitionSpec as P

DH = 64
ROWS = 4096
LAT = 2048
E = 512
C = 1024
PACK = 256
SMALL = 128
LARGE = 272
TB = 256
CH = 1024
ROW_PARTS = 4
MEM_PARTS = 4
CHUNK = 128 + 64 + 32 + 8
f32 = jnp.float32
bf16 = jnp.bfloat16


def _dot(a, b, dims):
    return lax.dot_general(a, b, (dims, ((), ())), preferred_element_type=f32)


NN = ((1,), (0,))
NT = ((1,), (1,))


def main_kernel(
    sidx, masked_hbm, q_hbm, g_hbm, mem_hbm, wq_hbm, wk_hbm, wv_hbm, wo_hbm,
    keep, send,
    masked, q_in, g_in, mem, qc, gc, kv, wkv, wq2, wo2, pos, off_v, off_s,
    kvt, sc_s, dp_s, eb_s,
    dkv, wqo, wkv_out, wqo_out,
    mem_sem, row_sem, w_sem, off_sem,
):
    me = sidx[0]
    w_copies = [
        pltpu.make_async_copy(src, dst, w_sem.at[i])
        for i, (src, dst) in enumerate(
            (
                (wk_hbm, wkv.at[pl.ds(0, DH)]),
                (wv_hbm, wkv.at[pl.ds(DH, DH)]),
                (wq_hbm, wq2.at[pl.ds(0, DH)]),
                (wo_hbm, wo2.at[pl.ds(DH, DH)]),
            )
        )
    ]
    mrows = LAT // MEM_PARTS
    mem_parts = [pl.ds(i * mrows, mrows) for i in range(MEM_PARTS)]
    mem_copies = [
        pltpu.make_async_copy(mem_hbm.at[part], mem.at[part], mem_sem.at[i])
        for i, part in enumerate(mem_parts)
    ]
    rrows = ROWS // ROW_PARTS
    row_copies = [
        [
            pltpu.make_async_copy(
                src.at[pl.ds(i * rrows, rrows)], dst.at[pl.ds(i * rrows, rrows)], row_sem.at[2 * i + j]
            )
            for j, (src, dst) in enumerate(((q_hbm, q_in), (g_hbm, g_in)))
        ]
        for i in range(ROW_PARTS)
    ]
    mask_copy = pltpu.make_async_copy(masked_hbm, masked, off_sem)
    mask_copy.start()
    for c in w_copies[:2] + mem_copies + row_copies[0] + w_copies[2:]:
        c.start()

    mask_copy.wait()
    ones = masked[...].astype(f32)
    mb = ones.astype(bf16)
    r128 = lax.broadcasted_iota(jnp.int32, (128, 128), 0)
    c128 = lax.broadcasted_iota(jnp.int32, (128, 128), 1)
    before = (r128 < c128).astype(f32).astype(bf16)
    rank = _dot(mb, before, NN)
    counts = _dot(mb, jnp.ones((128, 128), bf16), NN)
    r40 = lax.broadcasted_iota(jnp.int32, (40, 32), 0)
    c40 = lax.broadcasted_iota(jnp.int32, (40, 32), 1)
    earlier = (c40 < r40).astype(f32).astype(bf16)
    offs = _dot(earlier, counts.astype(bf16), NN)
    off_v[...] = offs.astype(jnp.int32)
    off_copy = pltpu.make_async_copy(off_v, off_s, off_sem)
    off_copy.start()
    pos[...] = jnp.where(ones > 0.5, offs[:32] + rank, -1.0).astype(jnp.int32)

    dkv[...] = jnp.zeros_like(dkv)
    wqo[...] = jnp.zeros_like(wqo)
    qc[pl.ds(0, 16), :] = jnp.zeros((16, E), bf16)
    gc[pl.ds(0, 16), :] = jnp.zeros((16, E), bf16)

    wq2[DH:, :] = jnp.zeros((DH, E), bf16)
    wo2[:DH, :] = jnp.zeros((DH, E), bf16)
    for c in w_copies:
        c.wait()
    for i, c in enumerate(mem_copies):
        c.wait()
        if i == 0:
            for pair in row_copies[1:]:
                for later in pair:
                    later.start()
    for part in mem_parts:
        proj = _dot(mem[part, :], wkv[...], NT)
        kv[part, :] = proj.astype(bf16)
        kvt[:, part] = proj.T.astype(bf16)
    off_copy.wait()
    total = off_s[32, 0]

    def put(b, start, size):
        row = lax.broadcasted_iota(jnp.int32, (size, 128), 0) + start
        picks = [
            (row == pos[pl.ds(2 * b + half, 1), :]).astype(f32).astype(bf16) for half in range(2)
        ]
        pick = jnp.concatenate(picks, axis=1)
        src = pl.ds(b * PACK, PACK)
        first = pl.ds(start, 16)
        rest = pl.ds(pl.multiple_of(start + 16, 16), size - 16)
        for s_ref, d_ref in ((q_in, qc), (g_in, gc)):
            rows = _dot(pick, s_ref[src, :], NN)
            d_ref[first, :] = (rows[:16] + d_ref[first, :].astype(f32)).astype(bf16)
            d_ref[rest, :] = rows[16:].astype(bf16)

    per = rrows // PACK

    def place(b):
        base = off_s[2 * b, 0]
        start = pl.multiple_of((base // 16) * 16, 16)
        return start, off_s[2 * b + 2, 0] - start < SMALL

    for part, pair in enumerate(row_copies):
        for c in pair:
            c.wait()
        blocks = [(b, *place(b)) for b in range(part * per, (part + 1) * per)]
        few = functools.reduce(jnp.logical_and, [ok for _, _, ok in blocks])

        def small():
            for b, start, _ in blocks:
                put(b, start, SMALL)

        def large():
            for b, start, _ in blocks:
                put(b, start, LARGE)

        pl.when(few)(small)
        pl.when(jnp.logical_not(few))(large)

    tail = pl.ds(pl.multiple_of(((total + 15) // 16) * 16, 16), TB)
    qc[tail, :] = jnp.zeros((TB, E), bf16)
    gc[tail, :] = jnp.zeros((TB, E), bf16)

    half = lax.broadcasted_iota(jnp.int32, (TB, 128), 1) < DH
    none = jnp.zeros((DH, TB), bf16)
    parts = [slice(c * CH, (c + 1) * CH) for c in range(LAT // CH)]

    def fold(x, op):
        rows = [x[8 * k : 8 * (k + 1)] for k in range(x.shape[0] // 8)]
        while len(rows) > 1:
            rows = [op(a, b) for a, b in zip(rows[::2], rows[1::2])]
        return rows[0]

    def begin(i):
        rows = pl.ds(pl.multiple_of(i * TB, TB), TB)
        qp = _dot(qc[rows, :], wq2[...], NT).astype(bf16).astype(f32) * 0.125
        da = _dot(gc[rows, :], wo2[...], NT).astype(bf16).astype(f32)
        zt = (qp + da).T
        qt = jnp.concatenate([zt[:DH].astype(bf16), none], axis=0)
        gt = jnp.concatenate([none, zt[DH:].astype(bf16)], axis=0)
        return zt, qt, gt

    def scores(qt, part):
        score = _dot(kv[part, :], qt, NN)
        sc_s[part, :] = score
        return fold(score, jnp.maximum)

    def over(op, a, b):
        return b if a is None else op(a, b)

    zt0, qt0, gt0 = begin(0)
    top0 = None
    for part in parts:
        top0 = over(jnp.maximum, top0, scores(qt0, part))
        dp_s[part, :] = _dot(kv[part, :], gt0, NN)

    def block(i, carried, more=True):
        zt, top = carried
        zt_n, qt_n, gt_n = begin(i + 1) if more else (None, None, None)
        top = jnp.max(top, axis=0, keepdims=True)
        norm = att = dq = top_n = None
        for part in parts:
            e = jnp.exp(sc_s[part, :] - top)
            eb = e.astype(bf16)
            eb_s[part, :] = eb
            norm = over(jnp.add, norm, fold(e, jnp.add))
            att = over(jnp.add, att, _dot(kvt[DH:, part], eb, NN))
            if more:
                top_n = over(jnp.maximum, top_n, scores(qt_n, part))
        inv = 1.0 / jnp.sum(norm, axis=0, keepdims=True)
        att = (att * inv).astype(bf16).astype(f32)
        delta = jnp.sum(zt[DH:] * att, axis=0, keepdims=True)
        y = (zt * inv).T
        yk = jnp.where(half, y, 0.0).astype(bf16)
        yv = jnp.where(half, 0.0, y).astype(bf16)
        ykv = jnp.concatenate([yk, yv], axis=0)
        for part in parts:
            eb = eb_s[part, :]
            ds = (eb.astype(f32) * (dp_s[part, :] - delta)).astype(bf16)
            if more:
                dp_s[part, :] = _dot(kv[part, :], gt_n, NN)
            dq = over(jnp.add, dq, _dot(kvt[:DH, part], ds, NN))
            dkv[part, :] += _dot(jnp.concatenate([ds, eb], axis=1), ykv, NN)
        rows = pl.ds(pl.multiple_of(i * TB, TB), TB)
        xq = (dq * (inv * 0.125)).astype(bf16)
        wqo[:DH, :] += _dot(xq, qc[rows, :], NN)
        wqo[DH:, :] += _dot(att.astype(bf16), gc[rows, :], NN)
        return zt_n, top_n

    last = jnp.maximum((total + TB - 1) // TB - 1, 0)
    block(last, lax.fori_loop(0, last, block, (zt0, top0)), False)

    wkvt = _dot(dkv[...].T.astype(bf16), mem[...], NN)
    lane64 = lax.broadcasted_iota(jnp.int32, (64, 128), 1)
    for t in range(8):
        tk = wkvt[:DH, 128 * t : 128 * (t + 1)]
        tv = wkvt[DH:, 128 * t : 128 * (t + 1)]
        wkv_out[2 * t] = jnp.where(lane64 < DH, tk, pltpu.roll(tv, 64, 1))
        wkv_out[2 * t + 1] = jnp.where(lane64 < DH, pltpu.roll(tk, 64, 1), tv)
    lane32 = lax.broadcasted_iota(jnp.int32, (32, 128), 1)
    for t in range(4):
        cols = slice(128 * t, 128 * (t + 1))
        for u in range(4):
            chunk = None
            for k, lo in ((0, 0), (1, 64), (2, 32), (3, 96)):
                piece = wqo[lo : lo + 32, cols]
                shift = (32 * (k - u)) % 128
                piece = pltpu.roll(piece, shift, 1) if shift else piece
                chunk = piece if chunk is None else jnp.where(lane32 >= 32 * k, piece, chunk)
            wqo_out[4 * t + u] = chunk
    count = jnp.zeros((8, 128), f32) + total.astype(f32)
    core = me & 1
    for p in range(16):
        i, rc = p % 8, p // 8
        out = (keep, send)[rc]
        s = (i // 4) * 8 + (i % 4) * 2 + (core ^ rc)
        out[i, 0:128] = dkv[pl.ds(pl.multiple_of(s * 128, 128), 128), :]
        out[i, 128:192] = wkv_out[s]
        out[i, 192:224] = wqo_out[s]
        out[i, 224:232] = count


def in_hbm(x):
    return pltpu.with_memory_space_constraint(x, pltpu.HBM)


def in_vmem(x):
    return pltpu.with_memory_space_constraint(x, pltpu.VMEM)


def run_main(sidx, masked, queries, grads, memory, w_query, w_key, w_value, w_out):
    any_ = pl.BlockSpec(memory_space=pl.ANY)
    vm = pl.BlockSpec(memory_space=pltpu.VMEM)
    a = pltpu.VMEM((8, CHUNK, 128), f32)
    arrays = [in_hbm(x) for x in (queries, grads, memory, w_query, w_key, w_value, w_out)]
    pad = ROWS + LARGE + TB
    return pl.pallas_call(
        main_kernel,
        out_shape=(a, a),
        in_specs=[pl.BlockSpec(memory_space=pltpu.SMEM)] + [any_] * 8,
        out_specs=(vm,) * 2,
        scratch_shapes=[
            pltpu.VMEM((32, 128), jnp.int32),
            pltpu.VMEM((ROWS, E), bf16),
            pltpu.VMEM((ROWS, E), bf16),
            pltpu.VMEM((LAT, C), bf16),
            pltpu.VMEM((pad, E), bf16),
            pltpu.VMEM((pad, E), bf16),
            pltpu.VMEM((LAT, 128), bf16),
            pltpu.VMEM((128, C), bf16),
            pltpu.VMEM((128, E), bf16),
            pltpu.VMEM((128, E), bf16),
            pltpu.VMEM((32, 128), jnp.int32),
            pltpu.VMEM((40, 128), jnp.int32),
            pltpu.SMEM((40, 128), jnp.int32),
            pltpu.VMEM((128, LAT), bf16),
            pltpu.VMEM((LAT, TB), f32),
            pltpu.VMEM((LAT, TB), f32),
            pltpu.VMEM((LAT, TB), bf16),
            pltpu.VMEM((LAT, 128), f32),
            pltpu.VMEM((128, E), f32),
            pltpu.VMEM((16, 64, 128), f32),
            pltpu.VMEM((16, 32, 128), f32),
            pltpu.SemaphoreType.DMA((MEM_PARTS,)),
            pltpu.SemaphoreType.DMA((2 * ROW_PARTS,)),
            pltpu.SemaphoreType.DMA((4,)),
            pltpu.SemaphoreType.DMA(()),
        ],
        compiler_params=pltpu.CompilerParams(vmem_limit_bytes=48 * 1024 * 1024),
        cost_estimate=pl.CostEstimate(flops=10**10, bytes_accessed=14 * 2**20, transcendentals=10**7),
        name="masked_rows",
    )(sidx, in_hbm(masked), *arrays)


VM = pl.BlockSpec(memory_space=pltpu.VMEM)


def total_of(parts, rows):
    t = parts[0, rows]
    for k in range(1, parts.shape[0]):
        t = t + parts[k, rows]
    return t


def head_kernel(parts, wk, wv, out, rest):
    dt = total_of(parts, slice(0, 128)).astype(bf16)
    for c in range(8):
        cols = slice(128 * c, 128 * (c + 1))
        w = jnp.concatenate([wk[:, cols], wv[:, cols]], axis=0)
        out[c] = _dot(dt, w, NN)
    rest[...] = total_of(parts, slice(128, CHUNK))


def run_head(parts, wk_t, wv_t):
    return pl.pallas_call(
        head_kernel,
        out_shape=(pltpu.VMEM((8, 128, 128), f32), pltpu.VMEM((CHUNK - 128, 128), f32)),
        in_specs=[VM] * 3,
        out_specs=(VM,) * 2,
        name="memory_part",
    )(in_vmem(parts), in_vmem(wk_t), in_vmem(wv_t))


def weights_kernel(rest, gwq, gwk, gwv, gwo_t, scale_out):
    scale = 1.0 / rest[96:104, :]
    scale_out[...] = scale
    b = rest[0:96] * scale[0:1]
    kv_t = b[0:64].T
    gwk[...] = kv_t[:64]
    gwv[...] = kv_t[64:]
    qo_t = b[64:96].T
    gwq[...] = jnp.concatenate([qo_t[0:32], qo_t[64:96]], axis=1)
    gwo_t[...] = jnp.concatenate([qo_t[32:64], qo_t[96:128]], axis=1)


def run_weights(rest):
    small = jax.ShapeDtypeStruct((32, 64), f32)
    square = jax.ShapeDtypeStruct((64, 64), f32)
    return pl.pallas_call(
        weights_kernel,
        out_shape=(small, square, square, small, pltpu.VMEM((8, 128), f32)),
        in_specs=[VM],
        out_specs=(VM,) * 5,
        name="weight_parts",
    )(in_vmem(rest))


def last_kernel(parts, scale, gmem):
    gmem[...] = total_of(parts, slice(0, 128)) * scale[0:1]


def run_last(parts, scale):
    return pl.pallas_call(
        last_kernel,
        out_shape=jax.ShapeDtypeStruct((128, 128), f32),
        in_specs=[VM] * 2,
        out_specs=VM,
        name="grad_memory",
    )(in_vmem(parts), in_vmem(scale))


def swap(x, axis, bits):
    n = lax.axis_size(axis)
    return lax.ppermute(x, axis, [(i, i ^ bits) for i in range(n)])


def shards(queries, memory, w_query, w_key, w_value, w_out, grad_out, masked):
    seq = lax.axis_index("seq").astype(jnp.int32).reshape(1)
    wk_t, wv_t = w_key.T, w_value.T
    keep, send = run_main(
        seq, masked.reshape(32, 128), queries, grad_out, memory, w_query.T, wk_t, wv_t, w_out
    )
    groups = [[z * 8 + x * 2 + core for z in range(2) for x in range(4)] for core in range(2)]
    parts = lax.all_to_all(keep + swap(send, "seq", 1), "seq", 0, 0, axis_index_groups=groups)
    part, rest = run_head(parts, wk_t, wv_t)
    grad_wq, grad_wk, grad_wv, grad_wo_t, scale = run_weights(rest)
    grad_memory = run_last(lax.all_to_all(part, "head", 0, 0), scale)
    return (grad_wq, grad_wk, grad_wv, grad_wo_t.T, grad_memory)


def solution(mesh):
    return jax.shard_map(
        shards,
        mesh=mesh,
        in_specs=(
            P("seq", None),
            P(),
            P(None, "head"),
            P(None, "head"),
            P(None, "head"),
            P("head", None),
            P("seq", None),
            P("seq"),
        ),
        out_specs=(
            P("seq", "head"),
            P("seq", "head"),
            P("seq", "head"),
            P("head", "seq"),
            P("seq", "head"),
        ),
        check_vma=False,
    )
```

```python
import functools

import jax
import jax.numpy as jnp
from jax import lax
from jax.experimental import pallas as pl
from jax.experimental.pallas import tpu as pltpu
from jax.sharding import PartitionSpec as P

DH = 64
ROWS = 4096
LAT = 2048
E = 512
C = 1024
PACK = 256
SMALL = 128
LARGE = 272
TB = 256
CH = 256
ROW_PARTS = 4
MEM_PARTS = 4
CHUNK = 128 + 64 + 32 + 8
f32 = jnp.float32
bf16 = jnp.bfloat16


def _dot(a, b, dims):
    return lax.dot_general(a, b, (dims, ((), ())), preferred_element_type=f32)


NN = ((1,), (0,))
NT = ((1,), (1,))


def main_kernel(
    sidx, masked_hbm, q_hbm, g_hbm, mem_hbm, wq_hbm, wk_hbm, wv_hbm, wo_hbm,
    keep, send,
    masked, q_in, g_in, mem, qc, gc, kv, wkv, wq2, wo2, pos, off_v, off_s,
    kvt, sc_s, dp_s, eb_s,
    dkv, wqo, wkv_out, wqo_out,
    mem_sem, row_sem, w_sem, off_sem,
):
    me = sidx[0]
    w_copies = [
        pltpu.make_async_copy(src, dst, w_sem.at[i])
        for i, (src, dst) in enumerate(
            (
                (wk_hbm, wkv.at[pl.ds(0, DH)]),
                (wv_hbm, wkv.at[pl.ds(DH, DH)]),
                (wq_hbm, wq2),
                (wo_hbm, wo2),
            )
        )
    ]
    mrows = LAT // MEM_PARTS
    mem_parts = [pl.ds(i * mrows, mrows) for i in range(MEM_PARTS)]
    mem_copies = [
        pltpu.make_async_copy(mem_hbm.at[part], mem.at[part], mem_sem.at[i])
        for i, part in enumerate(mem_parts)
    ]
    rrows = ROWS // ROW_PARTS
    row_copies = [
        [
            pltpu.make_async_copy(
                src.at[pl.ds(i * rrows, rrows)], dst.at[pl.ds(i * rrows, rrows)], row_sem.at[2 * i + j]
            )
            for j, (src, dst) in enumerate(((q_hbm, q_in), (g_hbm, g_in)))
        ]
        for i in range(ROW_PARTS)
    ]
    mask_copy = pltpu.make_async_copy(masked_hbm, masked, off_sem)
    mask_copy.start()
    for c in w_copies[:2] + mem_copies + row_copies[0] + w_copies[2:]:
        c.start()

    mask_copy.wait()
    ones = masked[...].astype(f32)
    mb = ones.astype(bf16)
    r128 = lax.broadcasted_iota(jnp.int32, (128, 128), 0)
    c128 = lax.broadcasted_iota(jnp.int32, (128, 128), 1)
    before = (r128 < c128).astype(f32).astype(bf16)
    rank = _dot(mb, before, NN)
    counts = _dot(mb, jnp.ones((128, 128), bf16), NN)
    r40 = lax.broadcasted_iota(jnp.int32, (40, 32), 0)
    c40 = lax.broadcasted_iota(jnp.int32, (40, 32), 1)
    earlier = (c40 < r40).astype(f32).astype(bf16)
    offs = _dot(earlier, counts.astype(bf16), NN)
    off_v[...] = offs.astype(jnp.int32)
    off_copy = pltpu.make_async_copy(off_v, off_s, off_sem)
    off_copy.start()
    pos[...] = jnp.where(ones > 0.5, offs[:32] + rank, -1.0).astype(jnp.int32)

    dkv[...] = jnp.zeros_like(dkv)
    wqo[...] = jnp.zeros_like(wqo)
    qc[pl.ds(0, 16), :] = jnp.zeros((16, E), bf16)
    gc[pl.ds(0, 16), :] = jnp.zeros((16, E), bf16)

    for c in w_copies:
        c.wait()
    for i, c in enumerate(mem_copies):
        c.wait()
        if i == 0:
            for pair in row_copies[1:]:
                for later in pair:
                    later.start()
    for part in mem_parts:
        proj = _dot(mem[part, :], wkv[...], NT)
        kv[part, :] = proj.astype(bf16)
        kvt[:, part] = proj.T.astype(bf16)
    off_copy.wait()
    total = off_s[32, 0]

    def put(b, start, size):
        row = lax.broadcasted_iota(jnp.int32, (size, 128), 0) + start
        picks = [
            (row == pos[pl.ds(2 * b + half, 1), :]).astype(f32).astype(bf16) for half in range(2)
        ]
        pick = jnp.concatenate(picks, axis=1)
        src = pl.ds(b * PACK, PACK)
        first = pl.ds(start, 16)
        rest = pl.ds(pl.multiple_of(start + 16, 16), size - 16)
        for s_ref, d_ref in ((q_in, qc), (g_in, gc)):
            rows = _dot(pick, s_ref[src, :], NN)
            d_ref[first, :] = (rows[:16] + d_ref[first, :].astype(f32)).astype(bf16)
            d_ref[rest, :] = rows[16:].astype(bf16)

    per = rrows // PACK

    def place(b):
        base = off_s[2 * b, 0]
        start = pl.multiple_of((base // 16) * 16, 16)
        return start, off_s[2 * b + 2, 0] - start < SMALL

    for part, pair in enumerate(row_copies):
        for c in pair:
            c.wait()
        blocks = [(b, *place(b)) for b in range(part * per, (part + 1) * per)]
        few = functools.reduce(jnp.logical_and, [ok for _, _, ok in blocks])

        def small():
            for b, start, _ in blocks:
                put(b, start, SMALL)

        def large():
            for b, start, _ in blocks:
                put(b, start, LARGE)

        pl.when(few)(small)
        pl.when(jnp.logical_not(few))(large)

    tail = pl.ds(pl.multiple_of(((total + 15) // 16) * 16, 16), TB)
    qc[tail, :] = jnp.zeros((TB, E), bf16)
    gc[tail, :] = jnp.zeros((TB, E), bf16)

    half = lax.broadcasted_iota(jnp.int32, (TB, 128), 1) < DH
    none = jnp.zeros((DH, TB), bf16)
    parts = [slice(c * CH, (c + 1) * CH) for c in range(LAT // CH)]

    def fold(x, op):
        rows = [x[8 * k : 8 * (k + 1)] for k in range(x.shape[0] // 8)]
        while len(rows) > 1:
            rows = [op(a, b) for a, b in zip(rows[::2], rows[1::2])]
        return rows[0]

    def begin(i):
        rows = pl.ds(pl.multiple_of(i * TB, TB), TB)
        qt = (_dot(wq2[...], qc[rows, :], NT).astype(bf16).astype(f32) * 0.125).astype(bf16)
        gt = _dot(wo2[...], gc[rows, :], NT).astype(bf16)
        zt = jnp.concatenate([qt, gt], axis=0).astype(f32)
        qt = jnp.concatenate([qt, none], axis=0)
        gt = jnp.concatenate([none, gt], axis=0)
        return zt, qt, gt

    def scores(qt, part):
        score = _dot(kv[part, :], qt, NN)
        sc_s[part, :] = score
        return fold(score, jnp.maximum)

    def over(op, a, b):
        return b if a is None else op(a, b)

    zt0, qt0, gt0 = begin(0)
    top0 = None
    for part in parts:
        top0 = over(jnp.maximum, top0, scores(qt0, part))
        dp_s[part, :] = _dot(kv[part, :], gt0, NN)

    def block(i, carried, more=True):
        zt, top = carried
        zt_n, qt_n, gt_n = begin(i + 1) if more else (None, None, None)
        top = jnp.max(top, axis=0, keepdims=True)
        norm = att = dq = top_n = None
        for part in parts:
            e = jnp.exp(sc_s[part, :] - top)
            eb = e.astype(bf16)
            eb_s[part, :] = eb
            norm = over(jnp.add, norm, fold(e, jnp.add))
            att = over(jnp.add, att, _dot(kvt[DH:, part], eb, NN))
            if more:
                top_n = over(jnp.maximum, top_n, scores(qt_n, part))
        inv = 1.0 / jnp.sum(norm, axis=0, keepdims=True)
        att = (att * inv).astype(bf16).astype(f32)
        delta = jnp.sum(zt[DH:] * att, axis=0, keepdims=True)
        y = (zt * inv).T
        ykv = jnp.concatenate([jnp.where(half, y, 0.0), jnp.where(half, 0.0, y)], axis=0).astype(bf16)
        for part in parts:
            eb = eb_s[part, :]
            ds = (eb.astype(f32) * (dp_s[part, :] - delta)).astype(bf16)
            if more:
                dp_s[part, :] = _dot(kv[part, :], gt_n, NN)
            dq = over(jnp.add, dq, _dot(kvt[:DH, part], ds, NN))
            dkv[part, :] += _dot(jnp.concatenate([ds, eb], axis=1), ykv, NN)
        rows = pl.ds(pl.multiple_of(i * TB, TB), TB)
        xq = (dq * (inv * 0.125)).astype(bf16)
        wqo[:DH, :] += _dot(xq, qc[rows, :], NN)
        wqo[DH:, :] += _dot(att.astype(bf16), gc[rows, :], NN)
        return zt_n, top_n

    last = jnp.maximum((total + TB - 1) // TB - 1, 0)
    block(last, lax.fori_loop(0, last, block, (zt0, top0)), False)

    wkvt = _dot(dkv[...].T.astype(bf16), mem[...], NN)
    lane64 = lax.broadcasted_iota(jnp.int32, (64, 128), 1)
    for t in range(8):
        tk = wkvt[:DH, 128 * t : 128 * (t + 1)]
        tv = wkvt[DH:, 128 * t : 128 * (t + 1)]
        wkv_out[2 * t] = jnp.where(lane64 < DH, tk, pltpu.roll(tv, 64, 1))
        wkv_out[2 * t + 1] = jnp.where(lane64 < DH, pltpu.roll(tk, 64, 1), tv)
    lane32 = lax.broadcasted_iota(jnp.int32, (32, 128), 1)
    for t in range(4):
        cols = slice(128 * t, 128 * (t + 1))
        for u in range(4):
            chunk = None
            for k, lo in ((0, 0), (1, 64), (2, 32), (3, 96)):
                piece = wqo[lo : lo + 32, cols]
                shift = (32 * (k - u)) % 128
                piece = pltpu.roll(piece, shift, 1) if shift else piece
                chunk = piece if chunk is None else jnp.where(lane32 >= 32 * k, piece, chunk)
            wqo_out[4 * t + u] = chunk
    count = jnp.zeros((8, 128), f32) + total.astype(f32)
    core = me & 1
    for p in range(16):
        i, rc = p % 8, p // 8
        out = (keep, send)[rc]
        s = (i // 4) * 8 + (i % 4) * 2 + (core ^ rc)
        out[i, 0:128] = dkv[pl.ds(pl.multiple_of(s * 128, 128), 128), :]
        out[i, 128:192] = wkv_out[s]
        out[i, 192:224] = wqo_out[s]
        out[i, 224:232] = count


def in_hbm(x):
    return pltpu.with_memory_space_constraint(x, pltpu.HBM)


def in_vmem(x):
    return pltpu.with_memory_space_constraint(x, pltpu.VMEM)


def run_main(sidx, masked, queries, grads, memory, w_query, w_key, w_value, w_out):
    any_ = pl.BlockSpec(memory_space=pl.ANY)
    vm = pl.BlockSpec(memory_space=pltpu.VMEM)
    a = pltpu.VMEM((8, CHUNK, 128), f32)
    arrays = [in_hbm(x) for x in (queries, grads, memory, w_query, w_key, w_value, w_out)]
    pad = ROWS + LARGE + TB
    return pl.pallas_call(
        main_kernel,
        out_shape=(a, a),
        in_specs=[pl.BlockSpec(memory_space=pltpu.SMEM)] + [any_] * 8,
        out_specs=(vm,) * 2,
        scratch_shapes=[
            pltpu.VMEM((32, 128), jnp.int32),
            pltpu.VMEM((ROWS, E), bf16),
            pltpu.VMEM((ROWS, E), bf16),
            pltpu.VMEM((LAT, C), bf16),
            pltpu.VMEM((pad, E), bf16),
            pltpu.VMEM((pad, E), bf16),
            pltpu.VMEM((LAT, 128), bf16),
            pltpu.VMEM((128, C), bf16),
            pltpu.VMEM((DH, E), bf16),
            pltpu.VMEM((DH, E), bf16),
            pltpu.VMEM((32, 128), jnp.int32),
            pltpu.VMEM((40, 128), jnp.int32),
            pltpu.SMEM((40, 128), jnp.int32),
            pltpu.VMEM((128, LAT), bf16),
            pltpu.VMEM((LAT, TB), f32),
            pltpu.VMEM((LAT, TB), f32),
            pltpu.VMEM((LAT, TB), bf16),
            pltpu.VMEM((LAT, 128), f32),
            pltpu.VMEM((128, E), f32),
            pltpu.VMEM((16, 64, 128), f32),
            pltpu.VMEM((16, 32, 128), f32),
            pltpu.SemaphoreType.DMA((MEM_PARTS,)),
            pltpu.SemaphoreType.DMA((2 * ROW_PARTS,)),
            pltpu.SemaphoreType.DMA((4,)),
            pltpu.SemaphoreType.DMA(()),
        ],
        compiler_params=pltpu.CompilerParams(vmem_limit_bytes=48 * 1024 * 1024),
        cost_estimate=pl.CostEstimate(flops=10**10, bytes_accessed=14 * 2**20, transcendentals=10**7),
        name="masked_rows",
    )(sidx, in_hbm(masked), *arrays)


VM = pl.BlockSpec(memory_space=pltpu.VMEM)


def total_of(parts, rows):
    t = parts[0, rows]
    for k in range(1, parts.shape[0]):
        t = t + parts[k, rows]
    return t


def head_kernel(parts, wk, wv, out):
    dt = total_of(parts, slice(0, 128)).astype(bf16)
    for c in range(8):
        cols = slice(128 * c, 128 * (c + 1))
        w = jnp.concatenate([wk[:, cols], wv[:, cols]], axis=0)
        out[c] = _dot(dt, w, NN)


def run_head(parts, wk_t, wv_t):
    return pl.pallas_call(
        head_kernel,
        out_shape=pltpu.VMEM((8, 128, 128), f32),
        in_specs=[VM] * 3,
        out_specs=VM,
        name="memory_part",
    )(in_vmem(parts), in_vmem(wk_t), in_vmem(wv_t))


def weights_kernel(parts, gwq, gwk, gwv, gwo_t, scale_out):
    rest = total_of(parts, slice(128, CHUNK))
    scale = 1.0 / rest[96:104, :]
    scale_out[...] = scale
    b = rest[0:96] * scale[0:1]
    kv_t = b[0:64].T
    gwk[...] = kv_t[:64]
    gwv[...] = kv_t[64:]
    qo_t = b[64:96].T
    gwq[...] = jnp.concatenate([qo_t[0:32], qo_t[64:96]], axis=1)
    gwo_t[...] = jnp.concatenate([qo_t[32:64], qo_t[96:128]], axis=1)


def run_weights(parts):
    small = jax.ShapeDtypeStruct((32, 64), f32)
    square = jax.ShapeDtypeStruct((64, 64), f32)
    return pl.pallas_call(
        weights_kernel,
        out_shape=(small, square, square, small, pltpu.VMEM((8, 128), f32)),
        in_specs=[VM],
        out_specs=(VM,) * 5,
        name="weight_parts",
    )(in_vmem(parts))


def last_kernel(parts, scale, gmem):
    gmem[...] = total_of(parts, slice(0, 128)) * scale[0:1]


def run_last(parts, scale):
    return pl.pallas_call(
        last_kernel,
        out_shape=jax.ShapeDtypeStruct((128, 128), f32),
        in_specs=[VM] * 2,
        out_specs=VM,
        name="grad_memory",
    )(in_vmem(parts), in_vmem(scale))


def swap(x, axis, bits):
    n = lax.axis_size(axis)
    return lax.ppermute(x, axis, [(i, i ^ bits) for i in range(n)])


def shards(queries, memory, w_query, w_key, w_value, w_out, grad_out, masked):
    seq = lax.axis_index("seq").astype(jnp.int32).reshape(1)
    wk_t, wv_t = w_key.T, w_value.T
    keep, send = run_main(
        seq, masked.reshape(32, 128), queries, grad_out, memory, w_query.T, wk_t, wv_t, w_out
    )
    groups = [[z * 8 + x * 2 + core for z in range(2) for x in range(4)] for core in range(2)]
    parts = lax.all_to_all(keep + swap(send, "seq", 1), "seq", 0, 0, axis_index_groups=groups)
    part = run_head(parts, wk_t, wv_t)
    grad_wq, grad_wk, grad_wv, grad_wo_t, scale = run_weights(parts)
    grad_memory = run_last(lax.all_to_all(part, "head", 0, 0), scale)
    return (grad_wq, grad_wk, grad_wv, grad_wo_t.T, grad_memory)


def solution(mesh):
    return jax.shard_map(
        shards,
        mesh=mesh,
        in_specs=(
            P("seq", None),
            P(),
            P(None, "head"),
            P(None, "head"),
            P(None, "head"),
            P("head", None),
            P("seq", None),
            P("seq"),
        ),
        out_specs=(
            P("seq", "head"),
            P("seq", "head"),
            P("seq", "head"),
            P("head", "seq"),
            P("seq", "head"),
        ),
        check_vma=False,
    )
```

```python
import functools

import jax
import jax.numpy as jnp
from jax import lax
from jax.experimental import pallas as pl
from jax.experimental.pallas import tpu as pltpu
from jax.sharding import PartitionSpec as P

DH = 64
ROWS = 4096
LAT = 2048
E = 512
C = 1024
PACK = 256
SMALL = 128
LARGE = 272
TB = 256
CH = 128
ROW_PARTS = 4
MEM_PARTS = 4
CHUNK = 128 + 64 + 32 + 8
f32 = jnp.float32
bf16 = jnp.bfloat16


def _dot(a, b, dims):
    return lax.dot_general(a, b, (dims, ((), ())), preferred_element_type=f32)


NN = ((1,), (0,))
NT = ((1,), (1,))


def main_kernel(
    sidx, masked_hbm, q_hbm, g_hbm, mem_hbm, wq_hbm, wk_hbm, wv_hbm, wo_hbm,
    keep, send,
    masked, q_in, g_in, mem, qc, gc, kv, wkv, wq2, wo2, pos, off_v, off_s,
    kvt, sc_s, dp_s, eb_s,
    dkv, wqo, wkv_out, wqo_out,
    mem_sem, row_sem, w_sem, off_sem,
):
    me = sidx[0]
    w_copies = [
        pltpu.make_async_copy(src, dst, w_sem.at[i])
        for i, (src, dst) in enumerate(
            (
                (wk_hbm, wkv.at[pl.ds(0, DH)]),
                (wv_hbm, wkv.at[pl.ds(DH, DH)]),
                (wq_hbm, wq2),
                (wo_hbm, wo2),
            )
        )
    ]
    mrows = LAT // MEM_PARTS
    mem_parts = [pl.ds(i * mrows, mrows) for i in range(MEM_PARTS)]
    mem_copies = [
        pltpu.make_async_copy(mem_hbm.at[part], mem.at[part], mem_sem.at[i])
        for i, part in enumerate(mem_parts)
    ]
    rrows = ROWS // ROW_PARTS
    row_copies = [
        [
            pltpu.make_async_copy(
                src.at[pl.ds(i * rrows, rrows)], dst.at[pl.ds(i * rrows, rrows)], row_sem.at[2 * i + j]
            )
            for j, (src, dst) in enumerate(((q_hbm, q_in), (g_hbm, g_in)))
        ]
        for i in range(ROW_PARTS)
    ]
    mask_copy = pltpu.make_async_copy(masked_hbm, masked, off_sem)
    mask_copy.start()
    for c in w_copies[:2] + mem_copies + row_copies[0] + w_copies[2:]:
        c.start()

    mask_copy.wait()
    ones = masked[...].astype(f32)
    mb = ones.astype(bf16)
    r128 = lax.broadcasted_iota(jnp.int32, (128, 128), 0)
    c128 = lax.broadcasted_iota(jnp.int32, (128, 128), 1)
    before = (r128 < c128).astype(f32).astype(bf16)
    rank = _dot(mb, before, NN)
    counts = _dot(mb, jnp.ones((128, 128), bf16), NN)
    r40 = lax.broadcasted_iota(jnp.int32, (40, 32), 0)
    c40 = lax.broadcasted_iota(jnp.int32, (40, 32), 1)
    earlier = (c40 < r40).astype(f32).astype(bf16)
    offs = _dot(earlier, counts.astype(bf16), NN)
    off_v[...] = offs.astype(jnp.int32)
    off_copy = pltpu.make_async_copy(off_v, off_s, off_sem)
    off_copy.start()
    pos[...] = jnp.where(ones > 0.5, offs[:32] + rank, -1.0).astype(jnp.int32)

    dkv[...] = jnp.zeros_like(dkv)
    wqo[...] = jnp.zeros_like(wqo)
    qc[pl.ds(0, 16), :] = jnp.zeros((16, E), bf16)
    gc[pl.ds(0, 16), :] = jnp.zeros((16, E), bf16)

    for c in w_copies:
        c.wait()
    for i, c in enumerate(mem_copies):
        c.wait()
        if i == 0:
            for pair in row_copies[1:]:
                for later in pair:
                    later.start()
    for part in mem_parts:
        proj = _dot(mem[part, :], wkv[...], NT)
        kv[part, :] = proj.astype(bf16)
        kvt[:, part] = proj.T.astype(bf16)
    off_copy.wait()
    total = off_s[32, 0]

    def put(b, start, size):
        row = lax.broadcasted_iota(jnp.int32, (size, 128), 0) + start
        picks = [
            (row == pos[pl.ds(2 * b + half, 1), :]).astype(f32).astype(bf16) for half in range(2)
        ]
        pick = jnp.concatenate(picks, axis=1)
        src = pl.ds(b * PACK, PACK)
        first = pl.ds(start, 16)
        rest = pl.ds(pl.multiple_of(start + 16, 16), size - 16)
        for s_ref, d_ref in ((q_in, qc), (g_in, gc)):
            rows = _dot(pick, s_ref[src, :], NN)
            d_ref[first, :] = (rows[:16] + d_ref[first, :].astype(f32)).astype(bf16)
            d_ref[rest, :] = rows[16:].astype(bf16)

    per = rrows // PACK

    def place(b):
        base = off_s[2 * b, 0]
        start = pl.multiple_of((base // 16) * 16, 16)
        return start, off_s[2 * b + 2, 0] - start < SMALL

    for part, pair in enumerate(row_copies):
        for c in pair:
            c.wait()
        blocks = [(b, *place(b)) for b in range(part * per, (part + 1) * per)]
        few = functools.reduce(jnp.logical_and, [ok for _, _, ok in blocks])

        def small():
            for b, start, _ in blocks:
                put(b, start, SMALL)

        def large():
            for b, start, _ in blocks:
                put(b, start, LARGE)

        pl.when(few)(small)
        pl.when(jnp.logical_not(few))(large)

    tail = pl.ds(pl.multiple_of(((total + 15) // 16) * 16, 16), TB)
    qc[tail, :] = jnp.zeros((TB, E), bf16)
    gc[tail, :] = jnp.zeros((TB, E), bf16)

    half = lax.broadcasted_iota(jnp.int32, (TB, 128), 1) < DH
    none = jnp.zeros((DH, TB), bf16)
    parts = [slice(c * CH, (c + 1) * CH) for c in range(LAT // CH)]

    def fold(x, op):
        rows = [x[8 * k : 8 * (k + 1)] for k in range(x.shape[0] // 8)]
        while len(rows) > 1:
            rows = [op(a, b) for a, b in zip(rows[::2], rows[1::2])]
        return rows[0]

    def begin(i):
        rows = pl.ds(pl.multiple_of(i * TB, TB), TB)
        qt = (_dot(wq2[...], qc[rows, :], NT).astype(bf16).astype(f32) * 0.125).astype(bf16)
        gt = _dot(wo2[...], gc[rows, :], NT).astype(bf16)
        zt = jnp.concatenate([qt, gt], axis=0).astype(f32)
        qt = jnp.concatenate([qt, none], axis=0)
        gt = jnp.concatenate([none, gt], axis=0)
        return zt, qt, gt

    def scores(qt, part):
        score = _dot(kv[part, :], qt, NN)
        sc_s[part, :] = score
        return fold(score, jnp.maximum)

    def over(op, a, b):
        return b if a is None else op(a, b)

    zt0, qt0, gt0 = begin(0)
    top0 = None
    for part in parts:
        top0 = over(jnp.maximum, top0, scores(qt0, part))
        dp_s[part, :] = _dot(kv[part, :], gt0, NN)

    def block(i, carried, more=True):
        zt, top = carried
        zt_n, qt_n, gt_n = begin(i + 1) if more else (None, None, None)
        top = jnp.max(top, axis=0, keepdims=True)
        norm = att = dq = top_n = None
        for part in parts:
            e = jnp.exp(sc_s[part, :] - top)
            eb = e.astype(bf16)
            eb_s[part, :] = eb
            norm = over(jnp.add, norm, fold(e, jnp.add))
            att = over(jnp.add, att, _dot(kvt[DH:, part], eb, NN))
            if more:
                top_n = over(jnp.maximum, top_n, scores(qt_n, part))
        inv = 1.0 / jnp.sum(norm, axis=0, keepdims=True)
        att = (att * inv).astype(bf16).astype(f32)
        delta = jnp.sum(zt[DH:] * att, axis=0, keepdims=True)
        y = (zt * inv).T
        ykv = jnp.concatenate([jnp.where(half, y, 0.0), jnp.where(half, 0.0, y)], axis=0).astype(bf16)
        for part in parts:
            eb = eb_s[part, :]
            ds = (eb.astype(f32) * (dp_s[part, :] - delta)).astype(bf16)
            if more:
                dp_s[part, :] = _dot(kv[part, :], gt_n, NN)
            dq = over(jnp.add, dq, _dot(kvt[:DH, part], ds, NN))
            dkv[part, :] += _dot(jnp.concatenate([ds, eb], axis=1), ykv, NN)
        rows = pl.ds(pl.multiple_of(i * TB, TB), TB)
        xq = (dq * (inv * 0.125)).astype(bf16)
        wqo[:DH, :] += _dot(xq, qc[rows, :], NN)
        wqo[DH:, :] += _dot(att.astype(bf16), gc[rows, :], NN)
        return zt_n, top_n

    last = jnp.maximum((total + TB - 1) // TB - 1, 0)
    block(last, lax.fori_loop(0, last, block, (zt0, top0)), False)

    wkvt = _dot(dkv[...].T.astype(bf16), mem[...], NN)
    lane64 = lax.broadcasted_iota(jnp.int32, (64, 128), 1)
    for t in range(8):
        tk = wkvt[:DH, 128 * t : 128 * (t + 1)]
        tv = wkvt[DH:, 128 * t : 128 * (t + 1)]
        wkv_out[2 * t] = jnp.where(lane64 < DH, tk, pltpu.roll(tv, 64, 1))
        wkv_out[2 * t + 1] = jnp.where(lane64 < DH, pltpu.roll(tk, 64, 1), tv)
    lane32 = lax.broadcasted_iota(jnp.int32, (32, 128), 1)
    for t in range(4):
        cols = slice(128 * t, 128 * (t + 1))
        for u in range(4):
            chunk = None
            for k, lo in ((0, 0), (1, 64), (2, 32), (3, 96)):
                piece = wqo[lo : lo + 32, cols]
                shift = (32 * (k - u)) % 128
                piece = pltpu.roll(piece, shift, 1) if shift else piece
                chunk = piece if chunk is None else jnp.where(lane32 >= 32 * k, piece, chunk)
            wqo_out[4 * t + u] = chunk
    count = jnp.zeros((8, 128), f32) + total.astype(f32)
    core = me & 1
    for p in range(16):
        i, rc = p % 8, p // 8
        out = (keep, send)[rc]
        s = (i // 4) * 8 + (i % 4) * 2 + (core ^ rc)
        out[i, 0:128] = dkv[pl.ds(pl.multiple_of(s * 128, 128), 128), :]
        out[i, 128:192] = wkv_out[s]
        out[i, 192:224] = wqo_out[s]
        out[i, 224:232] = count


def in_hbm(x):
    return pltpu.with_memory_space_constraint(x, pltpu.HBM)


def in_vmem(x):
    return pltpu.with_memory_space_constraint(x, pltpu.VMEM)


def run_main(sidx, masked, queries, grads, memory, w_query, w_key, w_value, w_out):
    any_ = pl.BlockSpec(memory_space=pl.ANY)
    vm = pl.BlockSpec(memory_space=pltpu.VMEM)
    a = pltpu.VMEM((8, CHUNK, 128), f32)
    arrays = [in_hbm(x) for x in (queries, grads, memory, w_query, w_key, w_value, w_out)]
    pad = ROWS + LARGE + TB
    return pl.pallas_call(
        main_kernel,
        out_shape=(a, a),
        in_specs=[pl.BlockSpec(memory_space=pltpu.SMEM)] + [any_] * 8,
        out_specs=(vm,) * 2,
        scratch_shapes=[
            pltpu.VMEM((32, 128), jnp.int32),
            pltpu.VMEM((ROWS, E), bf16),
            pltpu.VMEM((ROWS, E), bf16),
            pltpu.VMEM((LAT, C), bf16),
            pltpu.VMEM((pad, E), bf16),
            pltpu.VMEM((pad, E), bf16),
            pltpu.VMEM((LAT, 128), bf16),
            pltpu.VMEM((128, C), bf16),
            pltpu.VMEM((DH, E), bf16),
            pltpu.VMEM((DH, E), bf16),
            pltpu.VMEM((32, 128), jnp.int32),
            pltpu.VMEM((40, 128), jnp.int32),
            pltpu.SMEM((40, 128), jnp.int32),
            pltpu.VMEM((128, LAT), bf16),
            pltpu.VMEM((LAT, TB), f32),
            pltpu.VMEM((LAT, TB), f32),
            pltpu.VMEM((LAT, TB), bf16),
            pltpu.VMEM((LAT, 128), f32),
            pltpu.VMEM((128, E), f32),
            pltpu.VMEM((16, 64, 128), f32),
            pltpu.VMEM((16, 32, 128), f32),
            pltpu.SemaphoreType.DMA((MEM_PARTS,)),
            pltpu.SemaphoreType.DMA((2 * ROW_PARTS,)),
            pltpu.SemaphoreType.DMA((4,)),
            pltpu.SemaphoreType.DMA(()),
        ],
        compiler_params=pltpu.CompilerParams(vmem_limit_bytes=48 * 1024 * 1024),
        cost_estimate=pl.CostEstimate(flops=10**10, bytes_accessed=14 * 2**20, transcendentals=10**7),
        name="masked_rows",
    )(sidx, in_hbm(masked), *arrays)


VM = pl.BlockSpec(memory_space=pltpu.VMEM)


def total_of(parts, rows):
    t = parts[0, rows]
    for k in range(1, parts.shape[0]):
        t = t + parts[k, rows]
    return t


def head_kernel(parts, wk, wv, out):
    dt = total_of(parts, slice(0, 128)).astype(bf16)
    for c in range(8):
        cols = slice(128 * c, 128 * (c + 1))
        w = jnp.concatenate([wk[:, cols], wv[:, cols]], axis=0)
        out[c] = _dot(dt, w, NN)


def run_head(parts, wk_t, wv_t):
    return pl.pallas_call(
        head_kernel,
        out_shape=pltpu.VMEM((8, 128, 128), f32),
        in_specs=[VM] * 3,
        out_specs=VM,
        name="memory_part",
    )(in_vmem(parts), in_vmem(wk_t), in_vmem(wv_t))


def weights_kernel(parts, gwq, gwk, gwv, gwo_t, scale_out):
    rest = total_of(parts, slice(128, CHUNK))
    scale = 1.0 / rest[96:104, :]
    scale_out[...] = scale
    b = rest[0:96] * scale[0:1]
    kv_t = b[0:64].T
    gwk[...] = kv_t[:64]
    gwv[...] = kv_t[64:]
    qo_t = b[64:96].T
    gwq[...] = jnp.concatenate([qo_t[0:32], qo_t[64:96]], axis=1)
    gwo_t[...] = jnp.concatenate([qo_t[32:64], qo_t[96:128]], axis=1)


def run_weights(parts):
    small = jax.ShapeDtypeStruct((32, 64), f32)
    square = jax.ShapeDtypeStruct((64, 64), f32)
    return pl.pallas_call(
        weights_kernel,
        out_shape=(small, square, square, small, pltpu.VMEM((8, 128), f32)),
        in_specs=[VM],
        out_specs=(VM,) * 5,
        name="weight_parts",
    )(in_vmem(parts))


def last_kernel(parts, scale, gmem):
    gmem[...] = total_of(parts, slice(0, 128)) * scale[0:1]


def run_last(parts, scale):
    return pl.pallas_call(
        last_kernel,
        out_shape=jax.ShapeDtypeStruct((128, 128), f32),
        in_specs=[VM] * 2,
        out_specs=VM,
        name="grad_memory",
    )(in_vmem(parts), in_vmem(scale))


def swap(x, axis, bits):
    n = lax.axis_size(axis)
    return lax.ppermute(x, axis, [(i, i ^ bits) for i in range(n)])


def shards(queries, memory, w_query, w_key, w_value, w_out, grad_out, masked):
    seq = lax.axis_index("seq").astype(jnp.int32).reshape(1)
    wk_t, wv_t = w_key.T, w_value.T
    keep, send = run_main(
        seq, masked.reshape(32, 128), queries, grad_out, memory, w_query.T, wk_t, wv_t, w_out
    )
    groups = [[z * 8 + x * 2 + core for z in range(2) for x in range(4)] for core in range(2)]
    parts = lax.all_to_all(keep + swap(send, "seq", 1), "seq", 0, 0, axis_index_groups=groups)
    part = run_head(parts, wk_t, wv_t)
    grad_wq, grad_wk, grad_wv, grad_wo_t, scale = run_weights(parts)
    grad_memory = run_last(lax.all_to_all(part, "head", 0, 0), scale)
    return (grad_wq, grad_wk, grad_wv, grad_wo_t.T, grad_memory)


def solution(mesh):
    return jax.shard_map(
        shards,
        mesh=mesh,
        in_specs=(
            P("seq", None),
            P(),
            P(None, "head"),
            P(None, "head"),
            P(None, "head"),
            P("head", None),
            P("seq", None),
            P("seq"),
        ),
        out_specs=(
            P("seq", "head"),
            P("seq", "head"),
            P("seq", "head"),
            P("head", "seq"),
            P("seq", "head"),
        ),
        check_vma=False,
    )
```
